256 devices in a mesh: scene: 8 (over y, core), blk: 32 (over x, z).
Axes of the slice: x: 4, y: 4, z: 8, core: 2. Of those that a mesh axis runs over, the one named last changes fastest.
Arguments:
- coarse_feat: bfloat16 [8, 128, 64, 256], P('scene', 'blk'), may hold values from -6 to 6
- coarse_nbr: int32 [8, 128, 4], P('scene', 'blk'), may hold values from -1 to 127, as said below
- fine_dest: int32 [8, 128], P('scene', 'blk'), may hold values from 0 to 127, as said below
- fine_nbr: int32 [8, 128, 4], P('scene', 'blk'), may hold values from -1 to 127, as said below
- skip: bfloat16 [8, 128, 512, 128], P('scene', 'blk'), may hold values from -12 to 12
- cotangent: bfloat16 [8, 128, 512, 128], P('scene', 'blk'), may hold values from -0.0078125 to 0.0078125
- w_coarse: bfloat16 [27, 256, 256], replicated, may hold values from -0.078125 to 0.078125
- w_up: bfloat16 [256, 128], replicated, may hold values from -0.375 to 0.375
- w_fine: bfloat16 [27, 128, 128], replicated, may hold values from -0.109375 to 0.109375
Outputs:
- fine_out: bfloat16 [8, 128, 512, 128], P('scene', 'blk')
- grad_fine: float32 [128, 27, 128], P('blk')
The draws below stay inside these ranges and needn't reach their ends.
Inputs may be any that keep to these rules, and one draw needn't show every extreme that they name: `coarse_nbr`: entry k of coarse block b is the coarse index of the block beside b's face k, or -1. Neighbours are mutual, and lie on b's own device along blk or on the device just before or after it. `fine_dest`: for each scene a permutation of 0 to 127. Of the blocks that one device along blk holds in coarse order, at most 1 go to any one device along blk in fine order (fine index // 4), and that many do for some pair of devices. Entry k of fine block f is the fine index of the block beside f's face k, or -1; fine_nbr[s, fine_dest[s, b], k] = fine_dest[s, coarse_nbr[s, b, k]] where that entry is not -1, else -1. Neighbours lie on f's own device along blk or on the device just before or after it.
All inputs are finite; a program needn't handle non-finite values.
Results may differ from the reference program's by a relative error of at most 0.0058.
Values may be sent and summed in bfloat16 or wider, within the bound.
A program may use at most 64 MiB of HBM per device.

```python
import jax
import jax.numpy as jnp
from jax import lax

CC = 256
CF = 128
CEDGE = 4
FEDGE = 8
BLK_DEV = 4
NB = 128
SCENES = 8
N_BLK = 32


def scene_layout(key, scene_index):
    devices = N_BLK
    per_device = BLK_DEV
    rounds = (per_device + devices - 1) // devices
    key_start, key_order, key_coarse, key_fine = jax.random.split(key, 4)
    first_shift = jnp.where(scene_index == 0, 1, jax.random.randint(key_start, (), 0, devices))
    second_shift = (first_shift + 1) % devices
    values = jnp.arange(rounds * devices, dtype=jnp.int32)
    scores = jax.random.randint(key_order, (rounds * devices,), 0, 1 << 20) * (rounds * devices) + values
    scores = jnp.where(values == first_shift, -4, scores)
    scores = jnp.where(values == second_shift, -3, scores)
    scores = jnp.where((scene_index == 0) & (values == devices // 2), -2, scores)
    scores = jnp.where((scene_index == 0) & (values == devices - 1), -1, scores)
    shifts = jnp.argsort(scores)[:per_device].astype(jnp.int32)
    row_index = jnp.arange(devices, dtype=jnp.int32)[:, None]
    column = (row_index + shifts[None, :]) % devices
    copy_index = jnp.broadcast_to((shifts // devices)[None, :], column.shape)
    row_full = jnp.broadcast_to(row_index, column.shape)
    slot_range = jnp.arange(per_device, dtype=jnp.int32)[None, :]
    coarse_scores = jax.random.randint(key_coarse, (devices, per_device), 0, 1 << 20) * per_device + slot_range
    coarse_slot = jnp.argsort(jnp.argsort(coarse_scores, axis=1), axis=1).astype(jnp.int32)
    fine_scores = jax.random.randint(key_fine, (devices, per_device), 0, 1 << 20) * per_device + slot_range
    fine_slot = jnp.argsort(jnp.argsort(fine_scores, axis=1), axis=1).astype(jnp.int32)
    coarse_id = row_full * per_device + coarse_slot
    fine_id = column * per_device + fine_slot[column, jnp.broadcast_to(slot_range, column.shape)]
    all_blocks = devices * per_device

    def neighbours(ident):
        board = jnp.full((rounds, devices + 2, devices + 2), -1, dtype=jnp.int32)
        board = board.at[copy_index, row_full + 1, column + 1].set(ident)
        across = row_full + 1
        along = column + 1
        return jnp.stack([board[copy_index, across - 1, along], board[copy_index, across + 1, along], board[copy_index, across, along - 1], board[copy_index, across, along + 1]], axis=-1)
    coarse_table = jnp.zeros((all_blocks, 4), jnp.int32).at[coarse_id.reshape(-1)].set(neighbours(coarse_id).reshape(-1, 4))
    destination = jnp.zeros((all_blocks,), jnp.int32).at[coarse_id.reshape(-1)].set(fine_id.reshape(-1))
    fine_table = jnp.zeros((all_blocks, 4), jnp.int32).at[fine_id.reshape(-1)].set(neighbours(fine_id).reshape(-1, 4))
    return (coarse_table, destination, fine_table)


def layout_tables(key):
    scene_keys = jax.random.split(jax.random.fold_in(key, 11), SCENES)
    return jax.vmap(scene_layout)(scene_keys, jnp.arange(SCENES, dtype=jnp.int32))


def draw_coarse_nbr(key, part):
    return layout_tables(key)[0].astype(jnp.int32)


def draw_fine_dest(key, part):
    return layout_tables(key)[1].astype(jnp.int32)


def draw_fine_nbr(key, part):
    return layout_tables(key)[2].astype(jnp.int32)


def spiked(entries, stream_key, source, target, shards_of, factor):
    owner, partner = [(jnp.arange(entries.shape[dim]) // (entries.shape[dim] // shards_of)).reshape([-1 if axis == dim else 1 for axis in range(entries.ndim)]) for dim in (source, target)]
    chosen = jax.random.permutation(stream_key, shards_of)[partner]
    strong = (owner == chosen) | (owner == (partner + shards_of // 2) % shards_of)
    return jnp.where(strong, factor * entries, entries)


def steps_of(rng, extent, cuts, least, high):
    def one(position, parts):
        heights = jax.random.uniform(jax.random.fold_in(jax.random.fold_in(rng, 6), position), (parts,), jnp.float32, least / len(cuts), high / len(cuts))
        return jnp.repeat(jnp.exp(heights), extent[position] // parts).reshape((-1,) + (1,) * (len(extent) - position - 1))

    gain = one(*cuts[0])
    for cut in cuts[1:]:
        gain = gain * one(*cut)
    return gain


def normal_values(stream_key, shape, spread, reach, shards=(), kind=jnp.bfloat16):
    entries = jax.random.normal(stream_key, shape, jnp.float32) * spread
    if len(shards) > 0:
        entries = steps_of(stream_key, shape, shards, -0.22, 0.18) * entries
    return jnp.clip(entries, min=-reach, max=reach).astype(kind)


def gaussian_with(own_key, dims, scale, bound, shards, heavy, kind=jnp.bfloat16):
    result = scale * jax.random.normal(own_key, dims, jnp.float32)
    if shards:
        result = result * steps_of(own_key, dims, shards, -0.22, 0.18)
    return jnp.clip(spiked(result, jax.random.fold_in(own_key, 3), *heavy), -bound, bound).astype(kind)


def setup_inputs(seed: int = 0) -> dict:
    key_of = jax.random.split(jax.random.key(seed), 10)
    return {
        "coarse_feat": normal_values(key_of[0], (SCENES, NB, CEDGE ** 3, CC), 1.0, 6.0, ((0, 8), (1, 32))),
        "coarse_nbr": draw_coarse_nbr(jax.random.fold_in(key_of[9], 71), 0),
        "fine_dest": draw_fine_dest(jax.random.fold_in(key_of[9], 71), 0),
        "fine_nbr": draw_fine_nbr(jax.random.fold_in(key_of[9], 71), 0),
        "skip": gaussian_with(key_of[4], (SCENES, NB, FEDGE ** 3, CF), 1.0, 12.0, ((0, 8), (1, 32)), (1, 3, 32, 2.75)),
        "cotangent": normal_values(key_of[5], (SCENES, NB, FEDGE ** 3, CF), ((FEDGE ** 3 * NB * SCENES) ** -0.5), 0.0078125, ((0, 8), (1, 32))),
        "w_coarse": normal_values(key_of[6], (27, CC, CC), (27 * CC) ** -0.5, 0.078125),
        "w_up": normal_values(key_of[7], (CC, CF), CC ** -0.5, 0.375),
        "w_fine": normal_values(key_of[8], (27, CF, CF), (27 * CF) ** -0.5, 0.109375),
    }


def upsample(block_cells, side_cells):
    block_count = block_cells.shape[0]
    channels = block_cells.shape[-1]
    cell_grid = block_cells.reshape(block_count, side_cells, side_cells, side_cells, channels)
    cell_grid = jnp.repeat(jnp.repeat(jnp.repeat(cell_grid, 2, axis=1), 2, axis=2), 2, axis=3)
    return cell_grid.reshape(block_count, 8 * side_cells ** 3, channels)


def facing_layers(cell_grid):
    return jnp.stack([cell_grid[:, -1], cell_grid[:, 0], cell_grid[:, :, -1], cell_grid[:, :, 0]], axis=1)


def pad_faces(cell_grid, layers):
    padded = jnp.pad(cell_grid, ((0, 0), (1, 1), (1, 1), (1, 1), (0, 0)))
    padded = padded.at[:, 0, 1:-1, 1:-1].set(layers[:, 0])
    padded = padded.at[:, -1, 1:-1, 1:-1].set(layers[:, 1])
    padded = padded.at[:, 1:-1, 0, 1:-1].set(layers[:, 2])
    padded = padded.at[:, 1:-1, -1, 1:-1].set(layers[:, 3])
    return padded


def gather_layers(layers, face_table):
    chosen = []
    for face_index in range(4):
        neighbour = face_table[:, face_index]
        present = neighbour >= 0
        fetched = jnp.take(layers[:, face_index], jnp.maximum(neighbour, 0), axis=0)
        chosen.append(jnp.where(present[:, None, None, None], fetched, jnp.zeros_like(fetched)))
    return jnp.stack(chosen, axis=1)


def convolve(padded, weight, side_cells):
    block_count = padded.shape[0]
    channels = padded.shape[-1]
    running = None
    for off_x in range(3):
        for off_y in range(3):
            stacked = jnp.concatenate(
                [padded[:, off_x:off_x + side_cells, off_y:off_y + side_cells, off_z:off_z + side_cells] for off_z in range(3)],
                axis=-1).reshape(block_count * side_cells ** 3, 3 * channels)
            first_tap = 9 * off_x + 3 * off_y
            product = jnp.dot(stacked, weight[first_tap:first_tap + 3].reshape(3 * channels, -1),
                              preferred_element_type=jnp.float32)
            running = product if running is None else running + product
    return running


def silu_slope(pre_value):
    sigmoid_value = jax.nn.sigmoid(pre_value)
    return sigmoid_value * (1.0 + pre_value * (1.0 - sigmoid_value))


def reference(coarse_feat, coarse_nbr, fine_dest, fine_nbr, skip, cotangent, w_coarse, w_up, w_fine):
    fine_chans = w_fine.shape[-1]

    def one_scene(inputs):
        features, coarse_table, destination, fine_table, skip_scene, cot_scene = inputs
        block_count = features.shape[0]
        coarse_grid = features.reshape(block_count, CEDGE, CEDGE, CEDGE, -1)
        coarse_padded = pad_faces(coarse_grid, gather_layers(facing_layers(coarse_grid), coarse_table))
        coarse_act = jax.nn.silu(convolve(coarse_padded, w_coarse, CEDGE)).astype(jnp.bfloat16)
        projected = jnp.dot(coarse_act, w_up, preferred_element_type=jnp.float32).astype(jnp.bfloat16)
        upsampled = upsample(projected.reshape(block_count, CEDGE ** 3, fine_chans), CEDGE)
        source = jnp.zeros((block_count,), jnp.int32).at[destination].set(jnp.arange(block_count, dtype=jnp.int32))
        placed = jnp.take(upsampled, source, axis=0)
        hidden = (placed.astype(jnp.float32) + skip_scene.astype(jnp.float32)).astype(jnp.bfloat16)
        fine_grid = hidden.reshape(block_count, FEDGE, FEDGE, FEDGE, fine_chans)
        fine_padded = pad_faces(fine_grid, gather_layers(facing_layers(fine_grid), fine_table))
        pre_fine = convolve(fine_padded, w_fine, FEDGE)
        fine_scene = jax.nn.silu(pre_fine).astype(jnp.bfloat16).reshape(block_count, FEDGE ** 3, fine_chans)
        delta_fine = (cot_scene.reshape(-1, fine_chans).astype(jnp.float32) * silu_slope(pre_fine)).astype(jnp.bfloat16)
        tap_terms = []
        for off_x in range(3):
            for off_y in range(3):
                for off_z in range(3):
                    piece = fine_padded[:, off_x:off_x + FEDGE, off_y:off_y + FEDGE, off_z:off_z + FEDGE].reshape(-1, fine_chans)
                    tap_terms.append(lax.dot_general(piece, delta_fine, (((0,), (0,)), ((), ())),
                                                     preferred_element_type=jnp.float32))
        return fine_scene, jnp.stack(tap_terms, axis=1)

    fine_all, grad_all = lax.map(one_scene, (coarse_feat, coarse_nbr, fine_dest, fine_nbr, skip, cotangent))
    return fine_all, jnp.sum(grad_all, axis=0)
```

```python
import functools

import jax
import jax.numpy as jnp
import numpy as np
from jax import lax
from jax.experimental import pallas as pl
from jax.experimental.pallas import tpu as pltpu
from jax.sharding import PartitionSpec as P

MESH = pl.DeviceIdType.MESH
BLOCKS = 4
LINES = 16
TAPS = 27
CF = 128
CC = 256
BF16 = jnp.bfloat16
F32 = jnp.float32


def coarse_selector():
    rows = np.zeros((3, 3, 6, 4, 4, 256), np.float32)
    for q, r, px, y, z in np.ndindex(3, 3, 6, 4, 4):
        x, yy, zz = px - 1, y + q - 1, z + r - 1
        if not 0 <= zz < 4:
            continue
        inside = 0 <= yy < 4
        if x == -1 or x == 4:
            if inside:
                rows[q, r, px, y, z, (192 if x == -1 else 208) + 4 * yy + zz] = 1
        elif inside:
            rows[q, r, px, y, z, 16 * x + 4 * yy + zz] = 1
        elif yy == -1:
            rows[q, r, px, y, z, 64 + 16 * x + 12 + zz] = 1
        else:
            rows[q, r, px, y, z, 128 + 16 * x + zz] = 1
    return rows.reshape(864, 256)


def line_order():
    order = np.arange(256).reshape(BLOCKS, LINES, 4).transpose(1, 0, 2).reshape(-1)
    return np.eye(256, dtype=np.float32)[order]


def doubled_rows():
    source = (np.arange(12)[:, None] * 4 + np.arange(8)[None, :] // 2).reshape(-1)
    return np.eye(48, dtype=np.float32)[source]


def shard_order(taps):
    order = np.arange(taps * CF).reshape(taps, CF).T.reshape(-1)
    return np.eye(taps * CF, dtype=np.float32)[order]


def kernel(
    n_blk,
    n_scene,
    group,
    feat,
    coarse_nbr,
    dest,
    fine_nbr,
    skip,
    cot,
    w_coarse,
    w_up,
    w_fine,
    sel_c,
    order_c,
    double_z,
    order_g,
    out,
    grad,
    ext,
    wc,
    wu,
    wf,
    skip_v,
    cot_v,
    sel_cv,
    order_cv,
    double_v,
    order_gv,
    cols_c,
    meta_src,
    meta,
    line_src,
    lines,
    sel,
    perm,
    got,
    up,
    faces,
    cols,
    delta_t,
    out_v,
    pair_src,
    pair_dst,
    y_src,
    y_dst,
    shard_src,
    shards,
    done_src,
    done,
    local_sem,
    halo_send,
    halo_recv,
    meta_send,
    meta_recv,
    line_send,
    line_recv,
    got_send,
    got_recv,
    pair_send,
    pair_recv,
    y_send,
    y_recv,
    shard_send,
    shard_recv,
    done_send,
    done_recv,
    out_sem,
):
    me = lax.axis_index("blk")
    scene = lax.axis_index("scene")
    core = lax.rem(scene, 2)
    row = scene // 2
    rows = n_scene // 2
    stride = n_blk // LINES
    odd = lax.rem(scene, stride)
    right = lax.rem(me + 1, n_blk)
    left = lax.rem(me + n_blk - 1, n_blk)
    is_mid = lax.rem(me, stride) == odd

    loads = [
        pltpu.make_async_copy(source, target, local_sem.at[index])
        for index, (source, target) in enumerate(
            (
                (feat.at[0], ext.at[pl.ds(BLOCKS, BLOCKS)]),
                (skip.at[0], skip_v),
                (sel_c, sel_cv),
                (w_coarse, wc),
                (w_up, wu),
                (order_c, order_cv),
                (double_z, double_v),
                (w_fine, wf),
                (cot.at[0], cot_v),
                (order_g, order_gv),
            )
        )
    ]
    for load in loads:
        load.start()
    (
        load_feat,
        load_skip,
        load_sel,
        load_wc,
        load_wu,
        load_order,
        load_double,
        load_wf,
        load_cot,
        load_gorder,
    ) = loads

    barrier = pltpu.get_barrier_semaphore()

    def greet_blk(k, carry):
        pl.semaphore_signal(
            barrier,
            inc=1,
            device_id={"blk": lax.rem(me + k, n_blk)},
            device_id_type=MESH,
        )
        return carry

    def greet_scene(k, carry):
        pl.semaphore_signal(
            barrier,
            inc=1,
            device_id={"scene": lax.rem(scene + k, n_scene)},
            device_id_type=MESH,
        )
        return carry

    lax.fori_loop(1, n_blk, greet_blk, 0)
    lax.fori_loop(1, n_scene, greet_scene, 0)

    message_row = lax.broadcasted_iota(jnp.int32, (16, CF), 0)
    owner_rows = lax.rem(message_row, 4)
    for b in range(BLOCKS):
        owner_rows = owner_rows + jnp.where(message_row // 4 == b, 4 * dest[0, b], 0)
    meta_src[...] = owner_rows

    pl.semaphore_wait(barrier, n_blk + n_scene - 2)

    def remote(source, target, send, recv, **where):
        return pltpu.make_async_remote_copy(
            src_ref=source,
            dst_ref=target,
            send_sem=send,
            recv_sem=recv,
            device_id=where,
            device_id_type=MESH,
        )

    feat_right = remote(
        feat.at[0], ext.at[pl.ds(0, BLOCKS)], halo_send.at[0], halo_recv.at[0], blk=right
    )
    feat_left = remote(
        feat.at[0], ext.at[pl.ds(2 * BLOCKS, BLOCKS)], halo_send.at[1], halo_recv.at[1], blk=left
    )
    feat_right.start()
    feat_left.start()

    def over_lines(action):
        def step(k, carry):
            line = lax.rem(me // stride + k, LINES)
            action(line, line * stride + odd)
            return carry

        lax.fori_loop(0, LINES, step, 0)

    def meta_copy(line, peer):
        return remote(meta_src, meta.at[me], meta_send.at[line], meta_recv, blk=peer)

    def send_meta(line, peer):
        @pl.when(peer == me)
        def _():
            pltpu.make_async_copy(meta_src, meta.at[me], meta_recv).start()

        @pl.when(peer != me)
        def _():
            meta_copy(line, peer).start()

    over_lines(send_meta)

    load_skip.wait()

    def gather_faces(b, carry):
        faces[BLOCKS + b, 0] = skip_v[b, pl.ds(448, 64)]
        faces[BLOCKS + b, 1] = skip_v[b, pl.ds(0, 64)]
        layers = [
            skip_v[b, pl.ds(64 * x, 64)].astype(F32).reshape(8, 8, CF) for x in range(8)
        ]
        for face, y in ((2, 7), (3, 0)):
            layer = jnp.concatenate([part[y] for part in layers], axis=0)
            faces[BLOCKS + b, face] = layer.astype(BF16)
        return carry

    lax.fori_loop(0, BLOCKS, gather_faces, 0)
    own_faces = faces.at[pl.ds(BLOCKS, BLOCKS)]
    faces_right = remote(
        own_faces, faces.at[pl.ds(0, BLOCKS)], halo_send.at[2], halo_recv.at[2], blk=right
    )
    faces_left = remote(
        own_faces, faces.at[pl.ds(2 * BLOCKS, BLOCKS)], halo_send.at[3], halo_recv.at[3], blk=left
    )
    faces_right.start()
    faces_left.start()

    first = (me - 1) * BLOCKS
    last_slot = 3 * BLOCKS - 1
    load_feat.wait()
    load_sel.wait()
    feat_right.wait_recv()
    feat_left.wait_recv()

    def coarse_columns(b, carry):
        def beside(face, start, size):
            index = coarse_nbr[0, b, face]
            slot = jnp.clip(index - first, 0, last_slot)
            values = ext[slot, pl.ds(start, size), :]
            return jnp.where(index >= 0, values, jnp.zeros_like(values))

        sources = jnp.concatenate(
            [
                ext[BLOCKS + b],
                beside(2, 0, 64),
                beside(3, 0, 64),
                beside(0, 48, 16),
                beside(1, 0, 16),
                jnp.zeros((32, CC), BF16),
            ],
            axis=0,
        )
        cols_c[b] = jnp.dot(sel_cv[...], sources, preferred_element_type=F32).astype(BF16)
        return carry

    lax.fori_loop(0, BLOCKS, coarse_columns, 0)
    load_wc.wait()
    coarse = None
    for p in range(3):
        left_side = jnp.concatenate(
            [
                cols_c[:, 96 * qr + 16 * p : 96 * qr + 16 * p + 64, :].reshape(256, CC)
                for qr in range(9)
            ],
            axis=1,
        )
        product = jnp.dot(
            left_side,
            wc[9 * p : 9 * p + 9].reshape(9 * CC, CC),
            preferred_element_type=F32,
        )
        coarse = product if coarse is None else coarse + product
    active = (coarse / (1.0 + jnp.exp(-coarse))).astype(BF16)
    load_wu.wait()
    load_order.wait()
    projected = jnp.dot(active, wu[...], preferred_element_type=F32).astype(BF16)
    line_src[...] = (
        jnp.dot(order_cv[...], projected, preferred_element_type=F32)
        .astype(BF16)
        .reshape(LINES, 16, CF)
    )

    def line_copy(line, peer):
        return remote(line_src.at[line], lines.at[me], line_send.at[line], line_recv, blk=peer)

    def send_line(line, peer):
        @pl.when(peer == me)
        def _():
            pltpu.make_async_copy(line_src.at[line], lines.at[me], line_recv).start()

        @pl.when(peer != me)
        def _():
            line_copy(line, peer).start()

    over_lines(send_line)

    total = n_blk * 16
    my_line = me // stride

    def owner_copy(peer):
        return remote(
            perm.at[pl.ds(16 * peer, 48)],
            got.at[my_line],
            got_send.at[peer],
            got_recv,
            blk=peer,
        )

    @pl.when(is_mid)
    def _():
        pltpu.make_async_copy(meta, meta, meta_recv).wait()
        wanted = meta[...].reshape(total, CF)
        lane = lax.broadcasted_iota(jnp.int32, (total, CF), 1)
        for part in range(total // CF):
            hit = jnp.where(wanted == lane + part * CF, 1.0, 0.0)
            sel[part * CF : (part + 1) * CF, :] = hit.T.astype(BF16)
        perm[0:16, :] = jnp.zeros((16, CF), BF16)
        perm[total + 16 : total + 32, :] = jnp.zeros((16, CF), BF16)
        pltpu.make_async_copy(lines, lines, line_recv).wait()
        perm[16 : total + 16, :] = jnp.dot(
            sel[...], lines[...].reshape(total, CF), preferred_element_type=F32
        ).astype(BF16)
        pltpu.make_async_copy(perm.at[pl.ds(16 * me, 48)], got.at[my_line], got_recv).start()

        def step(k, carry):
            owner_copy(lax.rem(me + k, n_blk)).start()
            return carry

        lax.fori_loop(1, n_blk, step, 0)

    load_double.wait()
    load_wf.wait()
    load_cot.wait()
    faces_right.wait_recv()
    faces_left.wait_recv()
    pltpu.make_async_copy(got, got, got_recv).wait()

    def double_lines(line, carry):
        up[line] = jnp.dot(
            double_v[...], got[line], preferred_element_type=F32
        ).reshape(12, 8, CF)
        return carry

    lax.fori_loop(0, LINES, double_lines, 0)

    def fine_block(b, carry):
        def beside(face):
            index = fine_nbr[0, b, face]
            slot = jnp.clip(index - first, 0, last_slot)
            skips = faces[slot, face].astype(F32).reshape(8, 8, CF)
            parts = []
            for step in range(8):
                half = step // 2
                line = (12 + half, half, 4 * half + 3, 4 * half)[face]
                parts.append(up[line, slot] + skips[step])
            layer = jnp.stack(parts, axis=0)
            return jnp.where(index >= 0, layer, jnp.zeros_like(layer))

        low_x, high_x, low_y, high_y = (beside(face) for face in range(4))
        edge = jnp.zeros((1, 8, CF), F32)
        z_index = lax.broadcasted_iota(jnp.int32, (10, 8, CF), 1)
        for px in range(10):
            if px == 0:
                layer = jnp.concatenate([edge, low_x, edge], axis=0)
            elif px == 9:
                layer = jnp.concatenate([edge, high_x, edge], axis=0)
            else:
                x = px - 1
                skips = skip_v[b, pl.ds(64 * x, 64)].astype(F32).reshape(8, 8, CF)
                own = [up[4 * (x // 2) + y // 2, BLOCKS + b] + skips[y] for y in range(8)]
                layer = jnp.stack([low_y[x]] + own + [high_y[x]], axis=0)
            shifted = (
                jnp.where(z_index == 0, 0.0, pltpu.roll(layer, 1, 1)),
                layer,
                jnp.where(z_index == 7, 0.0, pltpu.roll(layer, 7, 1)),
            )
            for q in range(3):
                for r in range(3):
                    cols[3 * q + r, b, px] = shifted[r][q : q + 8].reshape(64, CF).astype(BF16)
        pre = None
        for p in range(3):
            left_side = jnp.concatenate(
                [cols[qr, b, p : p + 8].reshape(512, CF) for qr in range(9)], axis=1
            )
            product = jnp.dot(
                left_side,
                wf[9 * p : 9 * p + 9].reshape(9 * CF, CF),
                preferred_element_type=F32,
            )
            pre = product if pre is None else pre + product
        sigma = 1.0 / (1.0 + jnp.exp(-pre))
        out_v[b] = (pre * sigma).astype(BF16)
        delta = cot_v[b].astype(F32) * (sigma * (1.0 + pre * (1.0 - sigma)))
        delta_t[b] = delta.T.astype(BF16)
        return carry

    lax.fori_loop(0, BLOCKS, fine_block, 0)
    write_out = pltpu.make_async_copy(out_v, out.at[0], out_sem)
    write_out.start()

    def group_terms(index):
        pairs = []
        for first_tap in range(0, group, 2):
            picked = []
            for tap in (first_tap, first_tap + 1):
                which = lax.rem(index * group + tap, TAPS)
                picked.append((which // 9, lax.rem(which, 9)))
            terms = None
            for b in range(BLOCKS):
                sides = jnp.concatenate(
                    [cols[qr, b, pl.ds(p, 8)].reshape(512, CF) for p, qr in picked], axis=1
                )
                product = jnp.dot(delta_t[b], sides, preferred_element_type=F32)
                terms = product if terms is None else terms + product
            pairs.append(terms)
        return jnp.concatenate(pairs, axis=1)

    def pair_copy(k):
        return remote(
            pair_src.at[k],
            pair_dst.at[k],
            pair_send.at[k],
            pair_recv.at[k],
            scene=scene + 1 - 2 * core,
        )

    def y_copy(k):
        return remote(
            y_src.at[k],
            y_dst.at[k],
            y_send.at[k],
            y_recv.at[k],
            scene=2 * lax.rem(row + 1 + k, rows) + core,
        )

    def for_partner(k, carry):
        pair_src[k] = group_terms(2 * lax.rem(row + 1 + k, rows) + 1 - core).astype(BF16)
        pair_copy(k).start()
        return carry

    lax.fori_loop(0, rows, for_partner, 0)

    def pair_sum(k):
        terms = group_terms(2 * lax.rem(row + 1 + k, rows) + core)
        pair_copy(k).wait_recv()
        return terms + pair_dst[k].astype(F32)

    def for_row(k, carry):
        y_src[k] = pair_sum(k).astype(BF16)
        y_copy(k).start()
        return carry

    lax.fori_loop(0, rows - 1, for_row, 0)
    scene_sum = pair_sum(rows - 1)
    for k in range(rows - 1):
        y_copy(k).wait_recv()
        scene_sum = scene_sum + y_dst[k].astype(F32)
    load_gorder.wait()
    ordered = lax.dot_general(
        order_gv[...],
        scene_sum.astype(BF16),
        (((1,), (1,)), ((), ())),
        preferred_element_type=F32,
    )
    shard_src[...] = ordered.astype(BF16).reshape(shard_src.shape)

    def shard_copy(k):
        peer = lax.rem(me + k, n_blk)
        return remote(
            shard_src.at[peer], shards.at[me], shard_send.at[peer], shard_recv, blk=peer
        )

    pltpu.make_async_copy(shard_src.at[me], shards.at[me], shard_recv).start()

    def send_shard(k, carry):
        shard_copy(k).start()
        return carry

    lax.fori_loop(1, n_blk, send_shard, 0)
    pltpu.make_async_copy(shards, shards, shard_recv).wait()
    done_src[...] = jnp.sum(shards[...].astype(F32), axis=0)

    def done_copy(k):
        peer = lax.rem(scene + k, n_scene)
        return remote(done_src, done.at[scene], done_send.at[peer], done_recv, scene=peer)

    pltpu.make_async_copy(done_src, done.at[scene], done_recv).start()

    def send_done(k, carry):
        done_copy(k).start()
        return carry

    lax.fori_loop(1, n_scene, send_done, 0)
    pltpu.make_async_copy(done, done, done_recv).wait()
    for index in range(n_scene):
        count = min(group, TAPS - index * group)
        if count <= 0:
            continue
        for channel in range(CF // n_blk):
            grad[channel, index * group : index * group + count, :] = done[
                index, channel * group : channel * group + count, :
            ]

    feat_right.wait_send()
    feat_left.wait_send()
    faces_right.wait_send()
    faces_left.wait_send()

    def sent_line(line, peer):
        @pl.when(peer != me)
        def _():
            meta_copy(line, peer).wait_send()
            line_copy(line, peer).wait_send()

    over_lines(sent_line)

    @pl.when(is_mid)
    def _():
        def step(k, carry):
            owner_copy(lax.rem(me + k, n_blk)).wait_send()
            return carry

        lax.fori_loop(1, n_blk, step, 0)

    for k in range(rows):
        pair_copy(k).wait_send()
    for k in range(rows - 1):
        y_copy(k).wait_send()

    def sent_shard(k, carry):
        shard_copy(k).wait_send()
        return carry

    lax.fori_loop(1, n_blk, sent_shard, 0)

    def sent_done(k, carry):
        done_copy(k).wait_send()
        return carry

    lax.fori_loop(1, n_scene, sent_done, 0)
    write_out.wait()


def body(n_blk, n_scene, feat, coarse_nbr, dest, fine_nbr, skip, cot, w_coarse, w_up, w_fine):
    group = 4 * -(-TAPS // (4 * n_scene))
    shard = CF // n_blk
    rows = n_scene // 2
    any_spec = pl.BlockSpec(memory_space=pl.ANY)
    smem_spec = pl.BlockSpec(memory_space=pltpu.SMEM)
    vmem_spec = pl.BlockSpec(memory_space=pltpu.VMEM)
    vmem = pltpu.VMEM
    dma = pltpu.SemaphoreType.DMA
    scratch = [
        vmem((3 * BLOCKS, 64, CC), BF16),
        vmem((TAPS, CC, CC), BF16),
        vmem((CC, CF), BF16),
        vmem((TAPS, CF, CF), BF16),
        vmem((BLOCKS, 512, CF), BF16),
        vmem((BLOCKS, 512, CF), BF16),
        vmem((864, 256), BF16),
        vmem((256, 256), BF16),
        vmem((96, 48), BF16),
        vmem((group * CF, group * CF), BF16),
        vmem((BLOCKS, 864, CC), BF16),
        vmem((16, CF), jnp.int32),
        vmem((n_blk, 16, CF), jnp.int32),
        vmem((LINES, 16, CF), BF16),
        vmem((n_blk, 16, CF), BF16),
        vmem((n_blk * 16, n_blk * 16), BF16),
        vmem((n_blk * 16 + 32, CF), BF16),
        vmem((LINES, 48, CF), BF16),
        vmem((LINES, 12, 8, CF), F32),
        vmem((3 * BLOCKS, 4, 64, CF), BF16),
        vmem((9, BLOCKS, 10, 64, CF), BF16),
        vmem((BLOCKS, CF, 512), BF16),
        vmem((BLOCKS, 512, CF), BF16),
        vmem((rows, CF, group * CF), BF16),
        vmem((rows, CF, group * CF), BF16),
        vmem((max(rows - 1, 1), CF, group * CF), BF16),
        vmem((max(rows - 1, 1), CF, group * CF), BF16),
        vmem((n_blk, shard * group, CF), BF16),
        vmem((n_blk, shard * group, CF), BF16),
        vmem((shard * group, CF), F32),
        vmem((n_scene, shard * group, CF), F32),
        dma((10,)),
        dma((4,)),
        dma((4,)),
        dma((LINES,)),
        dma,
        dma((LINES,)),
        dma,
        dma((n_blk,)),
        dma,
        dma((rows,)),
        dma((rows,)),
        dma((max(rows - 1, 1),)),
        dma((max(rows - 1, 1),)),
        dma((n_blk,)),
        dma,
        dma((n_scene,)),
        dma,
        dma,
    ]
    fine_out, gradient = pl.pallas_call(
        functools.partial(kernel, n_blk, n_scene, group),
        out_shape=(
            jax.ShapeDtypeStruct((1, BLOCKS, 512, CF), BF16),
            jax.ShapeDtypeStruct((shard, TAPS, CF), F32),
        ),
        in_specs=[any_spec, smem_spec, smem_spec, smem_spec] + [any_spec] * 9,
        out_specs=(any_spec, vmem_spec),
        scratch_shapes=scratch,
        compiler_params=pltpu.CompilerParams(
            collective_id=0, has_side_effects=True, vmem_limit_bytes=60 * 1024 * 1024
        ),
        name="decoder_level",
    )(
        feat,
        coarse_nbr,
        dest,
        fine_nbr,
        skip,
        cot,
        w_coarse,
        w_up,
        w_fine,
        jnp.asarray(coarse_selector(), BF16),
        jnp.asarray(line_order(), BF16),
        jnp.asarray(doubled_rows(), BF16),
        jnp.asarray(shard_order(group), BF16),
    )
    return fine_out, gradient


def solution(mesh):
    in_specs = (
        P("scene", "blk", None, None),
        P("scene", "blk", None),
        P("scene", "blk"),
        P("scene", "blk", None),
        P("scene", "blk", None, None),
        P("scene", "blk", None, None),
        P(),
        P(),
        P(),
    )
    out_specs = (P("scene", "blk", None, None), P("blk", None, None))
    return jax.shard_map(
        functools.partial(body, mesh.shape["blk"], mesh.shape["scene"]),
        mesh=mesh,
        in_specs=in_specs,
        out_specs=out_specs,
        check_vma=False,
    )
```

```python
import functools

import jax
import jax.numpy as jnp
import numpy as np
from jax import lax
from jax.experimental import pallas as pl
from jax.experimental.pallas import tpu as pltpu
from jax.sharding import PartitionSpec as P

MESH = pl.DeviceIdType.MESH
BLOCKS = 4
LINES = 16
TAPS = 27
CF = 128
CC = 256
BF16 = jnp.bfloat16
F32 = jnp.float32


def coarse_selector():
    rows = np.zeros((3, 3, 6, 4, 4, 256), np.float32)
    for q, r, px, y, z in np.ndindex(3, 3, 6, 4, 4):
        x, yy, zz = px - 1, y + q - 1, z + r - 1
        if not 0 <= zz < 4:
            continue
        inside = 0 <= yy < 4
        if x == -1 or x == 4:
            if inside:
                rows[q, r, px, y, z, (192 if x == -1 else 208) + 4 * yy + zz] = 1
        elif inside:
            rows[q, r, px, y, z, 16 * x + 4 * yy + zz] = 1
        elif yy == -1:
            rows[q, r, px, y, z, 64 + 16 * x + 12 + zz] = 1
        else:
            rows[q, r, px, y, z, 128 + 16 * x + zz] = 1
    return rows.reshape(864, 256)


def line_order():
    order = np.arange(256).reshape(BLOCKS, LINES, 4).transpose(1, 0, 2).reshape(-1)
    return np.eye(256, dtype=np.float32)[order]


def doubled_rows():
    source = (np.arange(12)[:, None] * 4 + np.arange(8)[None, :] // 2).reshape(-1)
    return np.eye(48, dtype=np.float32)[source]


def shard_order(taps):
    order = np.arange(taps * CF).reshape(taps, CF).T.reshape(-1)
    return np.eye(taps * CF, dtype=np.float32)[order]


def kernel(
    n_blk,
    n_scene,
    group,
    feat,
    coarse_nbr,
    dest,
    fine_nbr,
    skip,
    cot,
    w_coarse,
    w_up,
    w_fine,
    sel_c,
    order_c,
    double_z,
    order_g,
    out,
    done,
    ext,
    wc,
    wu,
    wf,
    skip_v,
    cot_v,
    sel_cv,
    order_cv,
    double_v,
    order_gv,
    cols_c,
    meta_src,
    meta,
    line_src,
    lines,
    sel,
    perm,
    got,
    up,
    faces,
    cols,
    delta_t,
    out_v,
    pair_src,
    pair_dst,
    y_src,
    y_dst,
    shard_src,
    shards,
    done_src,
    local_sem,
    halo_send,
    halo_recv,
    meta_send,
    meta_recv,
    line_send,
    line_recv,
    got_send,
    got_recv,
    pair_send,
    pair_recv,
    y_send,
    y_recv,
    shard_send,
    shard_recv,
    done_send,
    done_recv,
    out_sem,
):
    me = lax.axis_index("blk")
    scene = lax.axis_index("scene")
    core = lax.rem(scene, 2)
    row = scene // 2
    rows = n_scene // 2
    stride = n_blk // LINES
    odd = lax.rem(scene, stride)
    right = lax.rem(me + 1, n_blk)
    left = lax.rem(me + n_blk - 1, n_blk)
    is_mid = lax.rem(me, stride) == odd

    loads = [
        pltpu.make_async_copy(source, target, local_sem.at[index])
        for index, (source, target) in enumerate(
            (
                (feat.at[0], ext.at[pl.ds(BLOCKS, BLOCKS)]),
                (skip.at[0], skip_v),
                (sel_c, sel_cv),
                (w_coarse, wc),
                (w_up, wu),
                (order_c, order_cv),
                (double_z, double_v),
                (w_fine, wf),
                (cot.at[0], cot_v),
                (order_g, order_gv),
            )
        )
    ]
    for load in loads:
        load.start()
    (
        load_feat,
        load_skip,
        load_sel,
        load_wc,
        load_wu,
        load_order,
        load_double,
        load_wf,
        load_cot,
        load_gorder,
    ) = loads

    barrier = pltpu.get_barrier_semaphore()

    def greet_blk(k, carry):
        pl.semaphore_signal(
            barrier,
            inc=1,
            device_id={"blk": lax.rem(me + k, n_blk)},
            device_id_type=MESH,
        )
        return carry

    def greet_scene(k, carry):
        pl.semaphore_signal(
            barrier,
            inc=1,
            device_id={"scene": lax.rem(scene + k, n_scene)},
            device_id_type=MESH,
        )
        return carry

    for k in range(1, n_blk):
        greet_blk(k, 0)
    lax.fori_loop(1, n_scene, greet_scene, 0)

    message_row = lax.broadcasted_iota(jnp.int32, (16, CF), 0)
    owner_rows = lax.rem(message_row, 4)
    for b in range(BLOCKS):
        owner_rows = owner_rows + jnp.where(message_row // 4 == b, 4 * dest[0, b], 0)
    meta_src[...] = owner_rows

    pl.semaphore_wait(barrier, n_blk + n_scene - 2)

    def remote(source, target, send, recv, **where):
        return pltpu.make_async_remote_copy(
            src_ref=source,
            dst_ref=target,
            send_sem=send,
            recv_sem=recv,
            device_id=where,
            device_id_type=MESH,
        )

    feat_right = remote(
        feat.at[0], ext.at[pl.ds(0, BLOCKS)], halo_send.at[0], halo_recv.at[0], blk=right
    )
    feat_left = remote(
        feat.at[0], ext.at[pl.ds(2 * BLOCKS, BLOCKS)], halo_send.at[1], halo_recv.at[1], blk=left
    )
    feat_right.start()
    feat_left.start()

    def over_lines(action):
        def step(k, carry):
            line = lax.rem(me // stride + k, LINES)
            action(line, line * stride + odd)
            return carry

        for k in range(LINES):
            step(k, 0)

    def meta_copy(line, peer):
        return remote(meta_src, meta.at[me], meta_send.at[line], meta_recv, blk=peer)

    def send_meta(line, peer):
        @pl.when(peer == me)
        def _():
            pltpu.make_async_copy(meta_src, meta.at[me], meta_recv).start()

        @pl.when(peer != me)
        def _():
            meta_copy(line, peer).start()

    over_lines(send_meta)

    load_skip.wait()

    def gather_faces(b, carry):
        faces[BLOCKS + b, 0] = skip_v[b, pl.ds(448, 64)]
        faces[BLOCKS + b, 1] = skip_v[b, pl.ds(0, 64)]
        layers = [
            skip_v[b, pl.ds(64 * x, 64)].astype(F32).reshape(8, 8, CF) for x in range(8)
        ]
        for face, y in ((2, 7), (3, 0)):
            layer = jnp.concatenate([part[y] for part in layers], axis=0)
            faces[BLOCKS + b, face] = layer.astype(BF16)
        return carry

    lax.fori_loop(0, BLOCKS, gather_faces, 0)
    own_faces = faces.at[pl.ds(BLOCKS, BLOCKS)]
    faces_right = remote(
        own_faces, faces.at[pl.ds(0, BLOCKS)], halo_send.at[2], halo_recv.at[2], blk=right
    )
    faces_left = remote(
        own_faces, faces.at[pl.ds(2 * BLOCKS, BLOCKS)], halo_send.at[3], halo_recv.at[3], blk=left
    )

    first = (me - 1) * BLOCKS
    last_slot = 3 * BLOCKS - 1
    load_feat.wait()
    load_sel.wait()
    feat_right.wait_recv()
    feat_left.wait_recv()

    def coarse_columns(b, carry):
        def beside(face, start, size):
            index = coarse_nbr[0, b, face]
            slot = jnp.clip(index - first, 0, last_slot)
            values = ext[slot, pl.ds(start, size), :]
            return jnp.where(index >= 0, values, jnp.zeros_like(values))

        sources = jnp.concatenate(
            [
                ext[BLOCKS + b],
                beside(2, 0, 64),
                beside(3, 0, 64),
                beside(0, 48, 16),
                beside(1, 0, 16),
                jnp.zeros((32, CC), BF16),
            ],
            axis=0,
        )
        cols_c[b] = jnp.dot(sel_cv[...], sources, preferred_element_type=F32).astype(BF16)
        return carry

    lax.fori_loop(0, BLOCKS, coarse_columns, 0)
    load_wc.wait()
    coarse = None
    for p in range(3):
        left_side = jnp.concatenate(
            [
                cols_c[:, 96 * qr + 16 * p : 96 * qr + 16 * p + 64, :].reshape(256, CC)
                for qr in range(9)
            ],
            axis=1,
        )
        product = jnp.dot(
            left_side,
            wc[9 * p : 9 * p + 9].reshape(9 * CC, CC),
            preferred_element_type=F32,
        )
        coarse = product if coarse is None else coarse + product
    active = (coarse / (1.0 + jnp.exp(-coarse))).astype(BF16)
    load_wu.wait()
    load_order.wait()
    projected = jnp.dot(active, wu[...], preferred_element_type=F32).astype(BF16)
    line_src[...] = (
        jnp.dot(order_cv[...], projected, preferred_element_type=F32)
        .astype(BF16)
        .reshape(LINES, 16, CF)
    )

    def line_copy(line, peer):
        return remote(line_src.at[line], lines.at[me], line_send.at[line], line_recv, blk=peer)

    def send_line(line, peer):
        @pl.when(peer == me)
        def _():
            pltpu.make_async_copy(line_src.at[line], lines.at[me], line_recv).start()

        @pl.when(peer != me)
        def _():
            line_copy(line, peer).start()

    over_lines(send_line)
    faces_right.start()
    faces_left.start()

    total = n_blk * 16
    my_line = me // stride

    def owner_copy(peer):
        return remote(
            perm.at[pl.ds(16 * peer, 48)],
            got.at[my_line],
            got_send.at[peer],
            got_recv,
            blk=peer,
        )

    @pl.when(is_mid)
    def _():
        pltpu.make_async_copy(meta, meta, meta_recv).wait()
        wanted = meta[...].reshape(total, CF)
        lane = lax.broadcasted_iota(jnp.int32, (total, CF), 1)
        for part in range(total // CF):
            hit = jnp.where(wanted == lane + part * CF, 1.0, 0.0)
            sel[part * CF : (part + 1) * CF, :] = hit.T.astype(BF16)
        perm[0:16, :] = jnp.zeros((16, CF), BF16)
        perm[total + 16 : total + 32, :] = jnp.zeros((16, CF), BF16)
        pltpu.make_async_copy(lines, lines, line_recv).wait()
        perm[16 : total + 16, :] = jnp.dot(
            sel[...], lines[...].reshape(total, CF), preferred_element_type=F32
        ).astype(BF16)
        pltpu.make_async_copy(perm.at[pl.ds(16 * me, 48)], got.at[my_line], got_recv).start()

        def step(k, carry):
            owner_copy(lax.rem(me + k, n_blk)).start()
            return carry

        for k in range(1, n_blk):
            step(k, 0)

    load_double.wait()
    load_wf.wait()
    load_cot.wait()
    faces_right.wait_recv()
    faces_left.wait_recv()
    pltpu.make_async_copy(got, got, got_recv).wait()

    def double_lines(line, carry):
        up[line] = jnp.dot(
            double_v[...], got[line], preferred_element_type=F32
        ).reshape(12, 8, CF)
        return carry

    for k in range(LINES):
        double_lines(k, 0)

    def fine_block(b, carry):
        def beside(face):
            index = fine_nbr[0, b, face]
            slot = jnp.clip(index - first, 0, last_slot)
            skips = faces[slot, face].astype(F32).reshape(8, 8, CF)
            parts = []
            for step in range(8):
                half = step // 2
                line = (12 + half, half, 4 * half + 3, 4 * half)[face]
                parts.append(up[line, slot] + skips[step])
            layer = jnp.stack(parts, axis=0)
            return jnp.where(index >= 0, layer, jnp.zeros_like(layer))

        low_x, high_x, low_y, high_y = (beside(face) for face in range(4))
        edge = jnp.zeros((1, 8, CF), F32)
        z_index = lax.broadcasted_iota(jnp.int32, (10, 8, CF), 1)
        for px in range(10):
            if px == 0:
                layer = jnp.concatenate([edge, low_x, edge], axis=0)
            elif px == 9:
                layer = jnp.concatenate([edge, high_x, edge], axis=0)
            else:
                x = px - 1
                skips = skip_v[b, pl.ds(64 * x, 64)].astype(F32).reshape(8, 8, CF)
                own = [up[4 * (x // 2) + y // 2, BLOCKS + b] + skips[y] for y in range(8)]
                layer = jnp.stack([low_y[x]] + own + [high_y[x]], axis=0)
            shifted = (
                jnp.where(z_index == 0, 0.0, pltpu.roll(layer, 1, 1)),
                layer,
                jnp.where(z_index == 7, 0.0, pltpu.roll(layer, 7, 1)),
            )
            for q in range(3):
                for r in range(3):
                    cols[3 * q + r, b, px] = shifted[r][q : q + 8].reshape(64, CF).astype(BF16)
        pre = None
        for p in range(3):
            left_side = jnp.concatenate(
                [cols[qr, b, p : p + 8].reshape(512, CF) for qr in range(9)], axis=1
            )
            product = jnp.dot(
                left_side,
                wf[9 * p : 9 * p + 9].reshape(9 * CF, CF),
                preferred_element_type=F32,
            )
            pre = product if pre is None else pre + product
        sigma = 1.0 / (1.0 + jnp.exp(-pre))
        out_v[b] = (pre * sigma).astype(BF16)
        delta = cot_v[b].astype(F32) * (sigma * (1.0 + pre * (1.0 - sigma)))
        delta_t[b] = delta.T.astype(BF16)
        return carry

    for b in range(BLOCKS):
        fine_block(b, 0)
    write_out = pltpu.make_async_copy(out_v, out.at[0], out_sem)
    write_out.start()

    def group_terms(index):
        pairs = []
        for first_tap in range(0, group, 2):
            picked = []
            for tap in (first_tap, first_tap + 1):
                which = lax.rem(index * group + tap, TAPS)
                picked.append((which // 9, lax.rem(which, 9)))
            terms = None
            for b in range(BLOCKS):
                sides = jnp.concatenate(
                    [cols[qr, b, pl.ds(p, 8)].reshape(512, CF) for p, qr in picked], axis=1
                )
                product = jnp.dot(delta_t[b], sides, preferred_element_type=F32)
                terms = product if terms is None else terms + product
            pairs.append(terms)
        return jnp.concatenate(pairs, axis=1)

    def pair_copy(k):
        return remote(
            pair_src.at[k],
            pair_dst.at[k],
            pair_send.at[k],
            pair_recv.at[k],
            scene=scene + 1 - 2 * core,
        )

    def y_copy(k):
        return remote(
            y_src.at[k],
            y_dst.at[k],
            y_send.at[k],
            y_recv.at[k],
            scene=2 * lax.rem(row + 1 + k, rows) + core,
        )

    def for_partner(k, carry):
        pair_src[k] = group_terms(2 * lax.rem(row + 1 + k, rows) + 1 - core).astype(BF16)
        pair_copy(k).start()
        return carry

    lax.fori_loop(0, rows, for_partner, 0)

    def pair_sum(k):
        terms = group_terms(2 * lax.rem(row + 1 + k, rows) + core)
        pair_copy(k).wait_recv()
        return terms + pair_dst[k].astype(F32)

    def for_row(k, carry):
        y_src[k] = pair_sum(k).astype(BF16)
        y_copy(k).start()
        return carry

    lax.fori_loop(0, rows - 1, for_row, 0)
    scene_sum = pair_sum(rows - 1)
    for k in range(rows - 1):
        y_copy(k).wait_recv()
        scene_sum = scene_sum + y_dst[k].astype(F32)
    load_gorder.wait()
    ordered = lax.dot_general(
        order_gv[...],
        scene_sum.astype(BF16),
        (((1,), (1,)), ((), ())),
        preferred_element_type=F32,
    )
    shard_src[...] = ordered.astype(BF16).reshape(shard_src.shape)

    def shard_copy(k):
        peer = lax.rem(me + k, n_blk)
        return remote(
            shard_src.at[peer], shards.at[me], shard_send.at[peer], shard_recv, blk=peer
        )

    pltpu.make_async_copy(shard_src.at[me], shards.at[me], shard_recv).start()

    def send_shard(k, carry):
        shard_copy(k).start()
        return carry

    for k in range(1, n_blk):
        send_shard(k, 0)
    pltpu.make_async_copy(shards, shards, shard_recv).wait()
    done_src[...] = jnp.sum(shards[...].astype(F32), axis=0)

    def done_copy(k):
        peer = lax.rem(scene + k, n_scene)
        return remote(done_src, done.at[scene], done_send.at[peer], done_recv, scene=peer)

    pltpu.make_async_copy(done_src, done.at[scene], done_recv).start()

    def send_done(k, carry):
        done_copy(k).start()
        return carry

    for k in range(1, n_scene):
        send_done(k, 0)
    pltpu.make_async_copy(done, done, done_recv).wait()
    feat_right.wait_send()
    feat_left.wait_send()
    faces_right.wait_send()
    faces_left.wait_send()

    def sent_line(line, peer):
        @pl.when(peer != me)
        def _():
            meta_copy(line, peer).wait_send()
            line_copy(line, peer).wait_send()

    over_lines(sent_line)

    @pl.when(is_mid)
    def _():
        def step(k, carry):
            owner_copy(lax.rem(me + k, n_blk)).wait_send()
            return carry

        for k in range(1, n_blk):
            step(k, 0)

    for k in range(rows):
        pair_copy(k).wait_send()
    for k in range(rows - 1):
        y_copy(k).wait_send()

    def sent_shard(k, carry):
        shard_copy(k).wait_send()
        return carry

    lax.fori_loop(1, n_blk, sent_shard, 0)

    def sent_done(k, carry):
        done_copy(k).wait_send()
        return carry

    lax.fori_loop(1, n_scene, sent_done, 0)
    write_out.wait()


def assemble(group, level_out, shares, out, grad, shares_v, out_v, grad_v, in_sem, out_sem, grad_sem):
    load = pltpu.make_async_copy(shares, shares_v, grad_sem.at[0])
    reads = [
        pltpu.make_async_copy(level_out.at[0, b], out_v.at[b], in_sem.at[b])
        for b in range(BLOCKS)
    ]
    writes = [
        pltpu.make_async_copy(out_v.at[b], out.at[0, b], out_sem.at[b]) for b in range(BLOCKS)
    ]
    load.start()
    for read in reads:
        read.start()
    load.wait()
    for tap in range(TAPS):
        for channel in range(grad_v.shape[1]):
            grad_v[tap, channel, :] = shares_v[tap // group, channel * group + tap % group, :]
    store = pltpu.make_async_copy(grad_v, grad, grad_sem.at[1])
    store.start()
    for read, write in zip(reads, writes):
        read.wait()
        write.start()
    store.wait()
    for write in writes:
        write.wait()


def body(n_blk, n_scene, feat, coarse_nbr, dest, fine_nbr, skip, cot, w_coarse, w_up, w_fine):
    group = 4 * -(-TAPS // (4 * n_scene))
    shard = CF // n_blk
    rows = n_scene // 2
    any_spec = pl.BlockSpec(memory_space=pl.ANY)
    smem_spec = pl.BlockSpec(memory_space=pltpu.SMEM)
    vmem = pltpu.VMEM
    dma = pltpu.SemaphoreType.DMA
    scratch = [
        vmem((3 * BLOCKS, 64, CC), BF16),
        vmem((TAPS, CC, CC), BF16),
        vmem((CC, CF), BF16),
        vmem((TAPS, CF, CF), BF16),
        vmem((BLOCKS, 512, CF), BF16),
        vmem((BLOCKS, 512, CF), BF16),
        vmem((864, 256), BF16),
        vmem((256, 256), BF16),
        vmem((96, 48), BF16),
        vmem((group * CF, group * CF), BF16),
        vmem((BLOCKS, 864, CC), BF16),
        vmem((16, CF), jnp.int32),
        vmem((n_blk, 16, CF), jnp.int32),
        vmem((LINES, 16, CF), BF16),
        vmem((n_blk, 16, CF), BF16),
        vmem((n_blk * 16, n_blk * 16), BF16),
        vmem((n_blk * 16 + 32, CF), BF16),
        vmem((LINES, 48, CF), BF16),
        vmem((LINES, 12, 8, CF), F32),
        vmem((3 * BLOCKS, 4, 64, CF), BF16),
        vmem((9, BLOCKS, 10, 64, CF), BF16),
        vmem((BLOCKS, CF, 512), BF16),
        vmem((BLOCKS, 512, CF), BF16),
        vmem((rows, CF, group * CF), BF16),
        vmem((rows, CF, group * CF), BF16),
        vmem((max(rows - 1, 1), CF, group * CF), BF16),
        vmem((max(rows - 1, 1), CF, group * CF), BF16),
        vmem((n_blk, shard * group, CF), BF16),
        vmem((n_blk, shard * group, CF), BF16),
        vmem((shard * group, CF), F32),
        dma((10,)),
        dma((4,)),
        dma((4,)),
        dma((LINES,)),
        dma,
        dma((LINES,)),
        dma,
        dma((n_blk,)),
        dma,
        dma((rows,)),
        dma((rows,)),
        dma((max(rows - 1, 1),)),
        dma((max(rows - 1, 1),)),
        dma((n_blk,)),
        dma,
        dma((n_scene,)),
        dma,
        dma,
    ]
    level_out, shares = pl.pallas_call(
        functools.partial(kernel, n_blk, n_scene, group),
        out_shape=(
            jax.ShapeDtypeStruct((1, BLOCKS, 512, CF), BF16),
            jax.ShapeDtypeStruct((n_scene, shard * group, CF), F32),
        ),
        in_specs=[any_spec, smem_spec, smem_spec, smem_spec] + [any_spec] * 9,
        out_specs=(any_spec, any_spec),
        scratch_shapes=scratch,
        compiler_params=pltpu.CompilerParams(
            collective_id=0, has_side_effects=True, vmem_limit_bytes=60 * 1024 * 1024
        ),
        name="decoder_level",
    )(
        feat,
        coarse_nbr,
        dest,
        fine_nbr,
        skip,
        cot,
        w_coarse,
        w_up,
        w_fine,
        jnp.asarray(coarse_selector(), BF16),
        jnp.asarray(line_order(), BF16),
        jnp.asarray(doubled_rows(), BF16),
        jnp.asarray(shard_order(group), BF16),
    )
    fine_out, gradient = pl.pallas_call(
        functools.partial(assemble, group),
        out_shape=(
            jax.ShapeDtypeStruct((1, BLOCKS, 512, CF), BF16),
            jax.ShapeDtypeStruct((TAPS, shard, CF), F32),
        ),
        in_specs=[any_spec, any_spec],
        out_specs=(any_spec, any_spec),
        scratch_shapes=[
            vmem((n_scene, shard * group, CF), F32),
            vmem((BLOCKS, 512, CF), BF16),
            vmem((TAPS, shard, CF), F32),
            dma((BLOCKS,)),
            dma((BLOCKS,)),
            dma((2,)),
        ],
        name="assemble",
    )(level_out, shares)
    return fine_out, jnp.transpose(gradient, (1, 0, 2))


def solution(mesh):
    in_specs = (
        P("scene", "blk", None, None),
        P("scene", "blk", None),
        P("scene", "blk"),
        P("scene", "blk", None),
        P("scene", "blk", None, None),
        P("scene", "blk", None, None),
        P(),
        P(),
        P(),
    )
    out_specs = (P("scene", "blk", None, None), P("blk", None, None))
    return jax.shard_map(
        functools.partial(body, mesh.shape["blk"], mesh.shape["scene"]),
        mesh=mesh,
        in_specs=in_specs,
        out_specs=out_specs,
        check_vma=False,
    )
```

```python
import functools

import jax
import jax.numpy as jnp
import numpy as np
from jax import lax
from jax.experimental import pallas as pl
from jax.experimental.pallas import tpu as pltpu
from jax.sharding import PartitionSpec as P

MESH = pl.DeviceIdType.MESH
BLOCKS = 4
LINES = 16
TAPS = 27
DEPTH = 8
REST = 48
CF = 128
CC = 256
BF16 = jnp.bfloat16
F32 = jnp.float32


def coarse_selector():
    rows = np.zeros((3, 3, 6, 4, 4, 256), np.float32)
    for q, r, px, y, z in np.ndindex(3, 3, 6, 4, 4):
        x, yy, zz = px - 1, y + q - 1, z + r - 1
        if not 0 <= zz < 4:
            continue
        inside = 0 <= yy < 4
        if x == -1 or x == 4:
            if inside:
                rows[q, r, px, y, z, (192 if x == -1 else 208) + 4 * yy + zz] = 1
        elif inside:
            rows[q, r, px, y, z, 16 * x + 4 * yy + zz] = 1
        elif yy == -1:
            rows[q, r, px, y, z, 64 + 16 * x + 12 + zz] = 1
        else:
            rows[q, r, px, y, z, 128 + 16 * x + zz] = 1
    return rows.reshape(864, 256)


def line_order():
    order = np.arange(256).reshape(BLOCKS, LINES, 4).transpose(1, 0, 2).reshape(-1)
    return np.eye(256, dtype=np.float32)[order]


def doubled_rows():
    source = (np.arange(12)[:, None] * 4 + np.arange(8)[None, :] // 2).reshape(-1)
    return np.eye(48, dtype=np.float32)[source]


def shard_order(taps):
    order = np.arange(taps * CF).reshape(taps, CF).T.reshape(-1)
    return np.eye(taps * CF, dtype=np.float32)[order]


def kernel(
    n_blk,
    n_scene,
    group,
    feat,
    coarse_nbr,
    dest,
    fine_nbr,
    skip,
    cot,
    w_coarse,
    w_up,
    w_fine,
    sel_c,
    order_c,
    double_z,
    order_g,
    out,
    done,
    ext,
    wc,
    wu,
    wf,
    skip_v,
    cot_v,
    sel_cv,
    order_cv,
    double_v,
    order_gv,
    cols_c,
    meta_src,
    meta,
    line_src,
    lines,
    sel,
    perm,
    got,
    up,
    faces,
    cols,
    deltas,
    delta_t,
    out_v,
    rest,
    own,
    pair_src,
    pair_dst,
    plane_src,
    plane_dst,
    shard_src,
    shards,
    done_src,
    local_sem,
    halo_send,
    halo_recv,
    meta_send,
    meta_recv,
    line_send,
    line_recv,
    got_send,
    got_recv,
    pair_send,
    pair_recv,
    plane_send,
    plane_recv,
    shard_send,
    shard_recv,
    done_send,
    done_recv,
    out_sem,
    round_sem,
):
    me = lax.axis_index("blk")
    scene = lax.axis_index("scene")
    core = lax.rem(scene, 2)
    row = scene // 2
    rows = n_scene // 2
    n_x, n_z = n_blk // DEPTH, DEPTH
    my_x, my_z = me // n_z, lax.rem(me, n_z)
    stride = n_blk // LINES
    odd = lax.rem(scene, stride)
    right = lax.rem(me + 1, n_blk)
    left = lax.rem(me + n_blk - 1, n_blk)
    is_mid = lax.rem(me, stride) == odd

    loads = [
        pltpu.make_async_copy(source, target, local_sem.at[index])
        for index, (source, target) in enumerate(
            (
                (feat.at[0], ext.at[pl.ds(BLOCKS, BLOCKS)]),
                (skip.at[0], skip_v),
                (sel_c, sel_cv),
                (w_coarse, wc),
                (w_up, wu),
                (order_c, order_cv),
                (double_z, double_v),
                (w_fine, wf),
                (cot.at[0], cot_v),
                (order_g, order_gv),
            )
        )
    ]
    for load in loads:
        load.start()
    (
        load_feat,
        load_skip,
        load_sel,
        load_wc,
        load_wu,
        load_order,
        load_double,
        load_wf,
        load_cot,
        load_gorder,
    ) = loads

    barrier = pltpu.get_barrier_semaphore()

    def along(x=0, y=0, z=0, c=0):
        return {
            "blk": lax.rem(my_x + x, n_x) * n_z + lax.rem(my_z + z, n_z),
            "scene": 2 * lax.rem(row + y, rows) + lax.rem(core + c, 2),
        }

    def greet(semaphore, places):
        for place in places:
            pl.semaphore_signal(semaphore, inc=1, device_id=place, device_id_type=MESH)

    beside_me = [
        along(z=1),
        along(z=n_z - 1),
        along(x=1),
        along(x=n_x - 1),
        along(y=1),
        along(y=rows - 1),
    ]
    first_round = [{"blk": right}, {"blk": left}, along(c=1)] + beside_me
    later_rounds = [
        beside_me,
        [along(z=2), along(z=n_z - 2), along(c=1)],
        [along(x=x) for x in range(1, n_x)] + [along(y=y) for y in range(1, rows)],
    ]
    greet(barrier, first_round)

    message_row = lax.broadcasted_iota(jnp.int32, (16, CF), 0)
    owner_rows = lax.rem(message_row, 4)
    for b in range(BLOCKS):
        owner_rows = owner_rows + jnp.where(message_row // 4 == b, 4 * dest[0, b], 0)
    meta_src[...] = owner_rows

    pl.semaphore_wait(barrier, len(first_round))

    def remote(source, target, send, recv, **where):
        return pltpu.make_async_remote_copy(
            src_ref=source,
            dst_ref=target,
            send_sem=send,
            recv_sem=recv,
            device_id=where,
            device_id_type=MESH,
        )

    feat_right = remote(
        feat.at[0], ext.at[pl.ds(0, BLOCKS)], halo_send.at[0], halo_recv.at[0], blk=right
    )
    feat_left = remote(
        feat.at[0], ext.at[pl.ds(2 * BLOCKS, BLOCKS)], halo_send.at[1], halo_recv.at[1], blk=left
    )
    feat_right.start()
    feat_left.start()
    for index, places in enumerate(later_rounds):
        greet(round_sem.at[index], places)
        pl.semaphore_wait(round_sem.at[index], len(places))

    def over_lines(action):
        def step(k, carry):
            line = lax.rem(me // stride + k, LINES)
            action(line, line * stride + odd)
            return carry

        for k in range(LINES):
            step(k, 0)

    def meta_copy(line, peer):
        return remote(meta_src, meta.at[me], meta_send.at[line], meta_recv, blk=peer)

    def send_meta(line, peer):
        @pl.when(peer == me)
        def _():
            pltpu.make_async_copy(meta_src, meta.at[me], meta_recv).start()

        @pl.when(peer != me)
        def _():
            meta_copy(line, peer).start()

    over_lines(send_meta)

    load_skip.wait()

    def gather_faces(b, carry):
        faces[BLOCKS + b, 0] = skip_v[b, pl.ds(448, 64)]
        faces[BLOCKS + b, 1] = skip_v[b, pl.ds(0, 64)]
        layers = [
            skip_v[b, pl.ds(64 * x, 64)].astype(F32).reshape(8, 8, CF) for x in range(8)
        ]
        for face, y in ((2, 7), (3, 0)):
            layer = jnp.concatenate([part[y] for part in layers], axis=0)
            faces[BLOCKS + b, face] = layer.astype(BF16)
        return carry

    lax.fori_loop(0, BLOCKS, gather_faces, 0)
    own_faces = faces.at[pl.ds(BLOCKS, BLOCKS)]
    faces_right = remote(
        own_faces, faces.at[pl.ds(0, BLOCKS)], halo_send.at[2], halo_recv.at[2], blk=right
    )
    faces_left = remote(
        own_faces, faces.at[pl.ds(2 * BLOCKS, BLOCKS)], halo_send.at[3], halo_recv.at[3], blk=left
    )

    first = (me - 1) * BLOCKS
    last_slot = 3 * BLOCKS - 1
    load_feat.wait()
    load_sel.wait()
    feat_right.wait_recv()
    feat_left.wait_recv()

    def coarse_columns(b, carry):
        def beside(face, start, size):
            index = coarse_nbr[0, b, face]
            slot = jnp.clip(index - first, 0, last_slot)
            values = ext[slot, pl.ds(start, size), :]
            return jnp.where(index >= 0, values, jnp.zeros_like(values))

        sources = jnp.concatenate(
            [
                ext[BLOCKS + b],
                beside(2, 0, 64),
                beside(3, 0, 64),
                beside(0, 48, 16),
                beside(1, 0, 16),
                jnp.zeros((32, CC), BF16),
            ],
            axis=0,
        )
        cols_c[b] = jnp.dot(sel_cv[...], sources, preferred_element_type=F32).astype(BF16)
        return carry

    lax.fori_loop(0, BLOCKS, coarse_columns, 0)
    load_wc.wait()
    coarse = None
    for p in range(3):
        left_side = jnp.concatenate(
            [
                cols_c[:, 96 * qr + 16 * p : 96 * qr + 16 * p + 64, :].reshape(256, CC)
                for qr in range(9)
            ],
            axis=1,
        )
        product = jnp.dot(
            left_side,
            wc[9 * p : 9 * p + 9].reshape(9 * CC, CC),
            preferred_element_type=F32,
        )
        coarse = product if coarse is None else coarse + product
    active = (coarse / (1.0 + jnp.exp(-coarse))).astype(BF16)
    load_wu.wait()
    load_order.wait()
    projected = jnp.dot(active, wu[...], preferred_element_type=F32).astype(BF16)
    line_src[...] = (
        jnp.dot(order_cv[...], projected, preferred_element_type=F32)
        .astype(BF16)
        .reshape(LINES, 16, CF)
    )

    def line_copy(line, peer):
        return remote(line_src.at[line], lines.at[me], line_send.at[line], line_recv, blk=peer)

    def send_line(line, peer):
        @pl.when(peer == me)
        def _():
            pltpu.make_async_copy(line_src.at[line], lines.at[me], line_recv).start()

        @pl.when(peer != me)
        def _():
            line_copy(line, peer).start()

    over_lines(send_line)
    faces_right.start()
    faces_left.start()

    total = n_blk * 16
    my_line = me // stride

    def owner_copy(peer):
        return remote(
            perm.at[pl.ds(16 * peer, 48)],
            got.at[my_line],
            got_send.at[peer],
            got_recv,
            blk=peer,
        )

    @pl.when(is_mid)
    def _():
        pltpu.make_async_copy(meta, meta, meta_recv).wait()
        wanted = meta[...].reshape(total, CF)
        lane = lax.broadcasted_iota(jnp.int32, (total, CF), 1)
        for part in range(total // CF):
            hit = jnp.where(wanted == lane + part * CF, 1.0, 0.0)
            sel[part * CF : (part + 1) * CF, :] = hit.T.astype(BF16)
        perm[0:16, :] = jnp.zeros((16, CF), BF16)
        perm[total + 16 : total + 32, :] = jnp.zeros((16, CF), BF16)
        pltpu.make_async_copy(lines, lines, line_recv).wait()
        perm[16 : total + 16, :] = jnp.dot(
            sel[...], lines[...].reshape(total, CF), preferred_element_type=F32
        ).astype(BF16)
        pltpu.make_async_copy(perm.at[pl.ds(16 * me, 48)], got.at[my_line], got_recv).start()

        def step(k, carry):
            owner_copy(lax.rem(me + k, n_blk)).start()
            return carry

        for k in range(1, n_blk):
            step(k, 0)

    load_double.wait()
    load_wf.wait()
    load_cot.wait()
    faces_right.wait_recv()
    faces_left.wait_recv()
    pltpu.make_async_copy(got, got, got_recv).wait()

    def double_lines(line, carry):
        up[line] = jnp.dot(
            double_v[...], got[line], preferred_element_type=F32
        ).reshape(12, 8, CF)
        return carry

    for k in range(LINES):
        double_lines(k, 0)

    def fine_block(b, carry):
        def beside(face):
            index = fine_nbr[0, b, face]
            slot = jnp.clip(index - first, 0, last_slot)
            skips = faces[slot, face].astype(F32).reshape(8, 8, CF)
            parts = []
            for step in range(8):
                half = step // 2
                line = (12 + half, half, 4 * half + 3, 4 * half)[face]
                parts.append(up[line, slot] + skips[step])
            layer = jnp.stack(parts, axis=0)
            return jnp.where(index >= 0, layer, jnp.zeros_like(layer))

        low_x, high_x, low_y, high_y = (beside(face) for face in range(4))
        edge = jnp.zeros((1, 8, CF), F32)
        z_index = lax.broadcasted_iota(jnp.int32, (10, 8, CF), 1)
        for px in range(10):
            if px == 0:
                layer = jnp.concatenate([edge, low_x, edge], axis=0)
            elif px == 9:
                layer = jnp.concatenate([edge, high_x, edge], axis=0)
            else:
                x = px - 1
                skips = skip_v[b, pl.ds(64 * x, 64)].astype(F32).reshape(8, 8, CF)
                own = [up[4 * (x // 2) + y // 2, BLOCKS + b] + skips[y] for y in range(8)]
                layer = jnp.stack([low_y[x]] + own + [high_y[x]], axis=0)
            shifted = (
                jnp.where(z_index == 0, 0.0, pltpu.roll(layer, 1, 1)),
                layer,
                jnp.where(z_index == 7, 0.0, pltpu.roll(layer, 7, 1)),
            )
            for q in range(3):
                for r in range(3):
                    cols[3 * q + r, b // 2, px, b % 2] = shifted[r][q : q + 8].reshape(64, CF).astype(BF16)
        pre = None
        for p in range(3):
            left_side = jnp.concatenate(
                [cols[qr, b // 2, p : p + 8, b % 2].reshape(512, CF) for qr in range(9)], axis=1
            )
            product = jnp.dot(
                left_side,
                wf[9 * p : 9 * p + 9].reshape(9 * CF, CF),
                preferred_element_type=F32,
            )
            pre = product if pre is None else pre + product
        sigma = 1.0 / (1.0 + jnp.exp(-pre))
        out_v[b] = (pre * sigma).astype(BF16)
        delta = cot_v[b].astype(F32) * (sigma * (1.0 + pre * (1.0 - sigma)))
        deltas[b // 2, :, b % 2] = delta.reshape(8, 64, CF)
        return carry

    for b in range(BLOCKS):
        fine_block(b, 0)
    write_out = pltpu.make_async_copy(out_v, out.at[0], out_sem)
    write_out.start()

    for half in range(BLOCKS // 2):
        turned = deltas[half].reshape(1024, CF).T.astype(BF16)
        for p in range(3):
            rows_p = slice(CF * p, CF * (p + 1))
            if p > 0:
                delta_t[half, rows_p, : CF * p] = jnp.zeros((CF, CF * p), BF16)
            delta_t[half, rows_p, CF * p : CF * p + 1024] = turned
            if p < 2:
                delta_t[half, rows_p, CF * p + 1024 :] = jnp.zeros((CF, CF * (2 - p)), BF16)

    def terms_of(first, count):
        terms = None
        for half in range(BLOCKS // 2):
            sides = jnp.concatenate(
                [cols[first + j, half].reshape(1280, CF) for j in range(count)], axis=1
            )
            product = jnp.dot(delta_t[half], sides, preferred_element_type=F32)
            terms = product if terms is None else terms + product
        return terms

    def pair_copy(k):
        return remote(
            pair_src.at[k],
            pair_dst.at[k],
            pair_send.at[k],
            pair_recv.at[k],
            scene=scene + 1 - 2 * core,
        )

    load_gorder.wait()

    def plane_copy(k, j):
        peer_x = lax.rem(my_x + 1 + j, n_x)
        source = plane_src.at[k, pl.ds(pl.multiple_of(CF * peer_x, CF), CF)]
        target = plane_dst.at[my_x * rows + row]
        if k == rows - 1 and j == n_x - 1:
            return pltpu.make_async_copy(source, target, plane_recv)
        return remote(
            source,
            target,
            plane_send.at[k * n_x + j],
            plane_recv,
            blk=peer_x * n_z + my_z,
            scene=2 * lax.rem(row + 1 + k, rows) + core,
        )

    def send_plane(k):
        pair_copy(k).wait_recv()
        total_k = (own[k] + pair_dst[k].astype(F32)).astype(BF16)
        filled = jnp.concatenate([total_k[3 * CF :], jnp.zeros((CF - REST, CF), BF16)], axis=0)
        parts = [total_k[CF * p : CF * (p + 1)] for p in range(3)] + [filled]
        ordered = lax.dot_general(
            order_gv[...],
            jnp.concatenate(parts, axis=1),
            (((1,), (1,)), ((), ())),
            preferred_element_type=F32,
        )
        plane_src[k] = ordered.astype(BF16)
        for j in range(n_x):
            plane_copy(k, j).start()

    rest[...] = terms_of(8, 1)
    for k in range(rows):
        target = lax.rem(row + 1 + k, rows)
        terms = terms_of(2 * target, 2)
        low, high = terms[:, :CF], terms[:, CF:]

        def rest_of(member):
            return rest[pl.ds(pl.multiple_of(REST * member, 16), REST), :]

        pair_src[k, : 3 * CF] = jnp.where(core == 0, high, low).astype(BF16)
        pair_src[k, 3 * CF :] = rest_of(2 * target + 1 - core).astype(BF16)
        pair_copy(k).start()
        own[k, : 3 * CF] = jnp.where(core == 0, low, high)
        own[k, 3 * CF :] = rest_of(2 * target + core)
        if k > 1:
            send_plane(k - 2)
    send_plane(rows - 2)
    send_plane(rows - 1)
    pltpu.make_async_copy(plane_dst, plane_dst, plane_recv).wait()
    plane_sum = jnp.sum(plane_dst[...].astype(F32), axis=0)
    shard_src[...] = plane_sum.astype(BF16).reshape(shard_src.shape)

    def shard_copy(k):
        peer = lax.rem(my_z + k, n_z)
        return remote(
            shard_src.at[peer],
            shards.at[my_z],
            shard_send.at[peer],
            shard_recv,
            blk=my_x * n_z + peer,
        )

    for k in range(1, n_z):
        shard_copy(k).start()
    pltpu.make_async_copy(shard_src.at[my_z], shards.at[my_z], shard_recv).start()
    pltpu.make_async_copy(shards, shards, shard_recv).wait()
    done_src[...] = jnp.sum(shards[...].astype(F32), axis=0)

    def done_copy(k):
        peer = lax.rem(scene + k, n_scene)
        return remote(done_src, done.at[scene], done_send.at[peer], done_recv, scene=peer)

    pltpu.make_async_copy(done_src, done.at[scene], done_recv).start()

    def send_done(k, carry):
        done_copy(k).start()
        return carry

    for k in range(1, n_scene):
        send_done(k, 0)
    pltpu.make_async_copy(done, done, done_recv).wait()
    feat_right.wait_send()
    feat_left.wait_send()
    faces_right.wait_send()
    faces_left.wait_send()

    def sent_line(line, peer):
        @pl.when(peer != me)
        def _():
            meta_copy(line, peer).wait_send()
            line_copy(line, peer).wait_send()

    over_lines(sent_line)

    @pl.when(is_mid)
    def _():
        def step(k, carry):
            owner_copy(lax.rem(me + k, n_blk)).wait_send()
            return carry

        for k in range(1, n_blk):
            step(k, 0)

    for k in range(rows):
        pair_copy(k).wait_send()
    for k in range(rows):
        for j in range(n_x):
            if k < rows - 1 or j < n_x - 1:
                plane_copy(k, j).wait_send()
    for k in range(1, n_z):
        shard_copy(k).wait_send()

    def sent_done(k, carry):
        done_copy(k).wait_send()
        return carry

    lax.fori_loop(1, n_scene, sent_done, 0)
    write_out.wait()


def assemble(group, level_out, shares, out, grad, shares_v, out_v, grad_v, in_sem, out_sem, grad_sem):
    load = pltpu.make_async_copy(shares, shares_v, grad_sem.at[0])
    reads = [
        pltpu.make_async_copy(level_out.at[0, b], out_v.at[b], in_sem.at[b])
        for b in range(BLOCKS)
    ]
    writes = [
        pltpu.make_async_copy(out_v.at[b], out.at[0, b], out_sem.at[b]) for b in range(BLOCKS)
    ]
    load.start()
    for read in reads:
        read.start()
    load.wait()
    n_scene = shares_v.shape[0]
    for channel in range(grad_v.shape[1]):
        for p in range(3):
            for qr in range(n_scene):
                grad_v[9 * p + qr, channel, :] = shares_v[qr, channel * group + p, :]
        at = channel * group + 3
        last = jnp.concatenate(
            [shares_v[s, at : at + 1, :REST] for s in range(n_scene)], axis=1
        )
        for p in range(3):
            grad_v[9 * p + 8, channel : channel + 1, :] = last[:, CF * p : CF * (p + 1)]
    store = pltpu.make_async_copy(grad_v, grad, grad_sem.at[1])
    store.start()
    for read, write in zip(reads, writes):
        read.wait()
        write.start()
    store.wait()
    for write in writes:
        write.wait()


def body(n_blk, n_scene, feat, coarse_nbr, dest, fine_nbr, skip, cot, w_coarse, w_up, w_fine):
    group = 4
    shard = CF // n_blk
    rows = n_scene // 2
    n_x = n_blk // DEPTH
    any_spec = pl.BlockSpec(memory_space=pl.ANY)
    smem_spec = pl.BlockSpec(memory_space=pltpu.SMEM)
    vmem = pltpu.VMEM
    dma = pltpu.SemaphoreType.DMA
    scratch = [
        vmem((3 * BLOCKS, 64, CC), BF16),
        vmem((TAPS, CC, CC), BF16),
        vmem((CC, CF), BF16),
        vmem((TAPS, CF, CF), BF16),
        vmem((BLOCKS, 512, CF), BF16),
        vmem((BLOCKS, 512, CF), BF16),
        vmem((864, 256), BF16),
        vmem((256, 256), BF16),
        vmem((96, 48), BF16),
        vmem((group * CF, group * CF), BF16),
        vmem((BLOCKS, 864, CC), BF16),
        vmem((16, CF), jnp.int32),
        vmem((n_blk, 16, CF), jnp.int32),
        vmem((LINES, 16, CF), BF16),
        vmem((n_blk, 16, CF), BF16),
        vmem((n_blk * 16, n_blk * 16), BF16),
        vmem((n_blk * 16 + 32, CF), BF16),
        vmem((LINES, 48, CF), BF16),
        vmem((LINES, 12, 8, CF), F32),
        vmem((3 * BLOCKS, 4, 64, CF), BF16),
        vmem((9, BLOCKS // 2, 10, 2, 64, CF), BF16),
        vmem((BLOCKS // 2, 8, 2, 64, CF), F32),
        vmem((BLOCKS // 2, 3 * CF, 1280), BF16),
        vmem((BLOCKS, 512, CF), BF16),
        vmem((3 * CF, CF), F32),
        vmem((rows, 3 * CF + REST, CF), F32),
        vmem((rows, 3 * CF + REST, CF), BF16),
        vmem((rows, 3 * CF + REST, CF), BF16),
        vmem((rows, group * CF, CF), BF16),
        vmem((rows * n_x, group * CF // n_x, CF), BF16),
        vmem((DEPTH, shard * group, CF), BF16),
        vmem((DEPTH, shard * group, CF), BF16),
        vmem((shard * group, CF), F32),
        dma((10,)),
        dma((4,)),
        dma((4,)),
        dma((LINES,)),
        dma,
        dma((LINES,)),
        dma,
        dma((n_blk,)),
        dma,
        dma((rows,)),
        dma((rows,)),
        dma((rows * n_x,)),
        dma,
        dma((DEPTH,)),
        dma,
        dma((n_scene,)),
        dma,
        dma,
        pltpu.SemaphoreType.REGULAR((3,)),
    ]
    level_out, shares = pl.pallas_call(
        functools.partial(kernel, n_blk, n_scene, group),
        out_shape=(
            jax.ShapeDtypeStruct((1, BLOCKS, 512, CF), BF16),
            jax.ShapeDtypeStruct((n_scene, shard * group, CF), F32),
        ),
        in_specs=[any_spec, smem_spec, smem_spec, smem_spec] + [any_spec] * 9,
        out_specs=(any_spec, any_spec),
        scratch_shapes=scratch,
        compiler_params=pltpu.CompilerParams(
            collective_id=0, has_side_effects=True, vmem_limit_bytes=60 * 1024 * 1024
        ),
        name="decoder_level",
    )(
        feat,
        coarse_nbr,
        dest,
        fine_nbr,
        skip,
        cot,
        w_coarse,
        w_up,
        w_fine,
        jnp.asarray(coarse_selector(), BF16),
        jnp.asarray(line_order(), BF16),
        jnp.asarray(doubled_rows(), BF16),
        jnp.asarray(shard_order(group), BF16),
    )
    fine_out, gradient = pl.pallas_call(
        functools.partial(assemble, group),
        out_shape=(
            jax.ShapeDtypeStruct((1, BLOCKS, 512, CF), BF16),
            jax.ShapeDtypeStruct((TAPS, shard, CF), F32),
        ),
        in_specs=[any_spec, any_spec],
        out_specs=(any_spec, any_spec),
        scratch_shapes=[
            vmem((n_scene, shard * group, CF), F32),
            vmem((BLOCKS, 512, CF), BF16),
            vmem((TAPS, shard, CF), F32),
            dma((BLOCKS,)),
            dma((BLOCKS,)),
            dma((2,)),
        ],
        name="assemble",
    )(level_out, shares)
    return fine_out, jnp.transpose(gradient, (1, 0, 2))


def solution(mesh):
    in_specs = (
        P("scene", "blk", None, None),
        P("scene", "blk", None),
        P("scene", "blk"),
        P("scene", "blk", None),
        P("scene", "blk", None, None),
        P("scene", "blk", None, None),
        P(),
        P(),
        P(),
    )
    out_specs = (P("scene", "blk", None, None), P("blk", None, None))
    return jax.shard_map(
        functools.partial(body, mesh.shape["blk"], mesh.shape["scene"]),
        mesh=mesh,
        in_specs=in_specs,
        out_specs=out_specs,
        check_vma=False,
    )
```

```python
import functools

import jax
import jax.numpy as jnp
import numpy as np
from jax import lax
from jax.experimental import pallas as pl
from jax.experimental.pallas import tpu as pltpu
from jax.sharding import PartitionSpec as P

MESH = pl.DeviceIdType.MESH
BLOCKS = 4
LINES = 16
TAPS = 27
DEPTH = 8
REST = 48
CF = 128
CC = 256
BF16 = jnp.bfloat16
F32 = jnp.float32


def coarse_selector():
    rows = np.zeros((3, 3, 6, 4, 4, 256), np.float32)
    for q, r, px, y, z in np.ndindex(3, 3, 6, 4, 4):
        x, yy, zz = px - 1, y + q - 1, z + r - 1
        if not 0 <= zz < 4:
            continue
        inside = 0 <= yy < 4
        if x == -1 or x == 4:
            if inside:
                rows[q, r, px, y, z, (192 if x == -1 else 208) + 4 * yy + zz] = 1
        elif inside:
            rows[q, r, px, y, z, 16 * x + 4 * yy + zz] = 1
        elif yy == -1:
            rows[q, r, px, y, z, 64 + 16 * x + 12 + zz] = 1
        else:
            rows[q, r, px, y, z, 128 + 16 * x + zz] = 1
    return rows.reshape(864, 256)


def line_order():
    order = np.arange(256).reshape(BLOCKS, LINES, 4).transpose(1, 0, 2).reshape(-1)
    return np.eye(256, dtype=np.float32)[order]


def doubled_rows():
    source = (np.arange(12)[:, None] * 4 + np.arange(8)[None, :] // 2).reshape(-1)
    return np.eye(48, dtype=np.float32)[source]


def shard_order(taps):
    order = np.arange(taps * CF).reshape(taps, CF).T.reshape(-1)
    return np.eye(taps * CF, dtype=np.float32)[order]


def kernel(
    n_blk,
    n_scene,
    group,
    feat,
    coarse_nbr_in,
    dest_in,
    fine_nbr_in,
    skip,
    cot,
    w_coarse,
    w_up,
    w_fine,
    sel_c,
    order_c,
    double_z,
    order_g,
    out,
    done,
    coarse_nbr,
    dest,
    fine_nbr,
    ext,
    wc,
    wu,
    wf,
    skip_v,
    cot_v,
    sel_cv,
    order_cv,
    double_v,
    order_gv,
    cols_c,
    meta_src,
    meta,
    line_src,
    lines,
    sel,
    perm,
    got,
    up,
    faces,
    cols,
    deltas,
    delta_t,
    out_v,
    rest,
    own,
    pair_src,
    pair_dst,
    plane_src,
    plane_dst,
    shard_src,
    shards,
    done_src,
    local_sem,
    halo_send,
    halo_recv,
    meta_send,
    meta_recv,
    line_send,
    line_recv,
    got_send,
    got_recv,
    pair_send,
    pair_recv,
    plane_send,
    plane_recv,
    shard_send,
    shard_recv,
    done_send,
    done_recv,
    out_sem,
    round_sem,
):
    me = lax.axis_index("blk")
    scene = lax.axis_index("scene")
    core = lax.rem(scene, 2)
    row = scene // 2
    rows = n_scene // 2
    n_x, n_z = n_blk // DEPTH, DEPTH
    my_x, my_z = me // n_z, lax.rem(me, n_z)
    stride = n_blk // LINES
    odd = lax.rem(scene, stride)
    right = lax.rem(me + 1, n_blk)
    left = lax.rem(me + n_blk - 1, n_blk)
    is_mid = lax.rem(me, stride) == odd

    barrier = pltpu.get_barrier_semaphore()

    def along(x=0, y=0, z=0, c=0):
        return {
            "blk": lax.rem(my_x + x, n_x) * n_z + lax.rem(my_z + z, n_z),
            "scene": 2 * lax.rem(row + y, rows) + lax.rem(core + c, 2),
        }

    def greet(semaphore, places):
        for place in places:
            pl.semaphore_signal(semaphore, inc=1, device_id=place, device_id_type=MESH)

    beside_me = [
        along(z=1),
        along(z=n_z - 1),
        along(x=1),
        along(x=n_x - 1),
        along(y=1),
        along(y=rows - 1),
    ]
    first_round = [{"blk": right}, {"blk": left}, along(c=1)] + beside_me
    later_rounds = [
        beside_me,
        [along(z=2), along(z=n_z - 2), along(c=1)],
        [along(x=x) for x in range(1, n_x)] + [along(y=y) for y in range(1, rows)],
    ]
    greet(barrier, first_round)

    loads = [
        pltpu.make_async_copy(source, target, local_sem.at[index])
        for index, (source, target) in enumerate(
            (
                (feat.at[0], ext.at[pl.ds(BLOCKS, BLOCKS)]),
                (skip.at[0], skip_v),
                (sel_c, sel_cv),
                (w_coarse, wc),
                (w_up, wu),
                (order_c, order_cv),
                (double_z, double_v),
                (w_fine, wf),
                (cot.at[0], cot_v),
                (order_g, order_gv),
                (dest_in, dest),
                (coarse_nbr_in, coarse_nbr),
                (fine_nbr_in, fine_nbr),
            )
        )
    ]
    for load in loads:
        load.start()
    (
        load_feat,
        load_skip,
        load_sel,
        load_wc,
        load_wu,
        load_order,
        load_double,
        load_wf,
        load_cot,
        load_gorder,
        load_dest,
        load_coarse_nbr,
        load_fine_nbr,
    ) = loads

    pl.semaphore_wait(barrier, len(first_round))

    def remote(source, target, send, recv, **where):
        return pltpu.make_async_remote_copy(
            src_ref=source,
            dst_ref=target,
            send_sem=send,
            recv_sem=recv,
            device_id=where,
            device_id_type=MESH,
        )

    feat_right = remote(
        feat.at[0], ext.at[pl.ds(0, BLOCKS)], halo_send.at[0], halo_recv.at[0], blk=right
    )
    feat_left = remote(
        feat.at[0], ext.at[pl.ds(2 * BLOCKS, BLOCKS)], halo_send.at[1], halo_recv.at[1], blk=left
    )
    feat_right.start()
    feat_left.start()
    for index, places in enumerate(later_rounds):
        greet(round_sem.at[index], places)
        pl.semaphore_wait(round_sem.at[index], len(places))

    load_dest.wait()
    message_row = lax.broadcasted_iota(jnp.int32, (16, CF), 0)
    owner_rows = lax.rem(message_row, 4)
    for b in range(BLOCKS):
        owner_rows = owner_rows + jnp.where(message_row // 4 == b, 4 * dest[0, b], 0)
    meta_src[...] = owner_rows

    far_x, far_z = (2, 1, 3, 0), (4, 3, 5, 2, 6, 1, 7, 0)
    base_z = my_z + lax.rem(my_z + odd, stride)

    def over_lines(action):
        for dx in far_x:
            for dz in (4, 2, 6, 0):
                peer = lax.rem(my_x + dx, n_x) * n_z + lax.rem(base_z + dz, n_z)
                action(peer // stride, peer)

    def meta_copy(line, peer):
        return remote(meta_src, meta.at[me], meta_send.at[line], meta_recv, blk=peer)

    def send_meta(line, peer):
        @pl.when(peer == me)
        def _():
            pltpu.make_async_copy(meta_src, meta.at[me], meta_recv).start()

        @pl.when(peer != me)
        def _():
            meta_copy(line, peer).start()

    over_lines(send_meta)

    load_skip.wait()

    def gather_faces(b, carry):
        faces[BLOCKS + b, 0] = skip_v[b, pl.ds(448, 64)]
        faces[BLOCKS + b, 1] = skip_v[b, pl.ds(0, 64)]
        layers = [
            skip_v[b, pl.ds(64 * x, 64)].astype(F32).reshape(8, 8, CF) for x in range(8)
        ]
        for face, y in ((2, 7), (3, 0)):
            layer = jnp.concatenate([part[y] for part in layers], axis=0)
            faces[BLOCKS + b, face] = layer.astype(BF16)
        return carry

    lax.fori_loop(0, BLOCKS, gather_faces, 0)
    own_faces = faces.at[pl.ds(BLOCKS, BLOCKS)]
    faces_right = remote(
        own_faces, faces.at[pl.ds(0, BLOCKS)], halo_send.at[2], halo_recv.at[2], blk=right
    )
    faces_left = remote(
        own_faces, faces.at[pl.ds(2 * BLOCKS, BLOCKS)], halo_send.at[3], halo_recv.at[3], blk=left
    )

    first = (me - 1) * BLOCKS
    last_slot = 3 * BLOCKS - 1
    load_feat.wait()
    load_sel.wait()
    load_coarse_nbr.wait()
    feat_right.wait_recv()
    feat_left.wait_recv()

    def coarse_columns(b, carry):
        def beside(face, start, size):
            index = coarse_nbr[0, b, face]
            slot = jnp.clip(index - first, 0, last_slot)
            values = ext[slot, pl.ds(start, size), :]
            return jnp.where(index >= 0, values, jnp.zeros_like(values))

        sources = jnp.concatenate(
            [
                ext[BLOCKS + b],
                beside(2, 0, 64),
                beside(3, 0, 64),
                beside(0, 48, 16),
                beside(1, 0, 16),
                jnp.zeros((32, CC), BF16),
            ],
            axis=0,
        )
        cols_c[b] = jnp.dot(sel_cv[...], sources, preferred_element_type=F32).astype(BF16)
        return carry

    lax.fori_loop(0, BLOCKS, coarse_columns, 0)
    load_wc.wait()
    coarse = None
    for p in range(3):
        left_side = jnp.concatenate(
            [
                cols_c[:, 96 * qr + 16 * p : 96 * qr + 16 * p + 64, :].reshape(256, CC)
                for qr in range(9)
            ],
            axis=1,
        )
        product = jnp.dot(
            left_side,
            wc[9 * p : 9 * p + 9].reshape(9 * CC, CC),
            preferred_element_type=F32,
        )
        coarse = product if coarse is None else coarse + product
    active = (coarse / (1.0 + jnp.exp(-coarse))).astype(BF16)
    load_wu.wait()
    load_order.wait()
    projected = jnp.dot(active, wu[...], preferred_element_type=F32).astype(BF16)
    line_src[...] = (
        jnp.dot(order_cv[...], projected, preferred_element_type=F32)
        .astype(BF16)
        .reshape(LINES, 16, CF)
    )

    def line_copy(line, peer):
        return remote(line_src.at[line], lines.at[me], line_send.at[line], line_recv, blk=peer)

    def send_line(line, peer):
        @pl.when(peer == me)
        def _():
            pltpu.make_async_copy(line_src.at[line], lines.at[me], line_recv).start()

        @pl.when(peer != me)
        def _():
            line_copy(line, peer).start()

    over_lines(send_line)

    total = n_blk * 16
    my_line = me // stride

    def owner_copy(peer):
        return remote(
            perm.at[pl.ds(16 * peer, 48)],
            got.at[my_line],
            got_send.at[peer],
            got_recv,
            blk=peer,
        )

    @pl.when(is_mid)
    def _():
        pltpu.make_async_copy(meta, meta, meta_recv).wait()
        wanted = meta[...].reshape(total, CF)
        lane = lax.broadcasted_iota(jnp.int32, (total, CF), 1)
        for part in range(total // CF):
            hit = jnp.where(wanted == lane + part * CF, 1.0, 0.0)
            sel[part * CF : (part + 1) * CF, :] = hit.T.astype(BF16)
        perm[0:16, :] = jnp.zeros((16, CF), BF16)
        perm[total + 16 : total + 32, :] = jnp.zeros((16, CF), BF16)
        pltpu.make_async_copy(lines, lines, line_recv).wait()
        perm[16 : total + 16, :] = jnp.dot(
            sel[...], lines[...].reshape(total, CF), preferred_element_type=F32
        ).astype(BF16)
        pltpu.make_async_copy(perm.at[pl.ds(16 * me, 48)], got.at[my_line], got_recv).start()

        for dx in far_x:
            for dz in far_z:
                if dx or dz:
                    place = lax.rem(my_x + dx, n_x) * n_z + lax.rem(my_z + dz, n_z)
                    owner_copy(place).start()

    faces_right.start()
    faces_left.start()
    load_double.wait()
    load_fine_nbr.wait()
    load_wf.wait()
    load_cot.wait()
    faces_right.wait_recv()
    faces_left.wait_recv()
    pltpu.make_async_copy(got, got, got_recv).wait()

    def double_lines(line, carry):
        up[line] = jnp.dot(
            double_v[...], got[line], preferred_element_type=F32
        ).reshape(12, 8, CF)
        return carry

    for k in range(LINES):
        double_lines(k, 0)

    def fine_block(b, carry):
        def beside(face):
            index = fine_nbr[0, b, face]
            slot = jnp.clip(index - first, 0, last_slot)
            skips = faces[slot, face].astype(F32).reshape(8, 8, CF)
            parts = []
            for step in range(8):
                half = step // 2
                line = (12 + half, half, 4 * half + 3, 4 * half)[face]
                parts.append(up[line, slot] + skips[step])
            layer = jnp.stack(parts, axis=0)
            return jnp.where(index >= 0, layer, jnp.zeros_like(layer))

        low_x, high_x, low_y, high_y = (beside(face) for face in range(4))
        edge = jnp.zeros((1, 8, CF), F32)
        z_index = lax.broadcasted_iota(jnp.int32, (10, 8, CF), 1)
        for px in range(10):
            if px == 0:
                layer = jnp.concatenate([edge, low_x, edge], axis=0)
            elif px == 9:
                layer = jnp.concatenate([edge, high_x, edge], axis=0)
            else:
                x = px - 1
                skips = skip_v[b, pl.ds(64 * x, 64)].astype(F32).reshape(8, 8, CF)
                own = [up[4 * (x // 2) + y // 2, BLOCKS + b] + skips[y] for y in range(8)]
                layer = jnp.stack([low_y[x]] + own + [high_y[x]], axis=0)
            shifted = (
                jnp.where(z_index == 0, 0.0, pltpu.roll(layer, 1, 1)),
                layer,
                jnp.where(z_index == 7, 0.0, pltpu.roll(layer, 7, 1)),
            )
            for q in range(3):
                for r in range(3):
                    cols[3 * q + r, b // 2, px, b % 2] = shifted[r][q : q + 8].reshape(64, CF).astype(BF16)
        pre = None
        for p in range(3):
            left_side = jnp.concatenate(
                [cols[qr, b // 2, p : p + 8, b % 2].reshape(512, CF) for qr in range(9)], axis=1
            )
            product = jnp.dot(
                left_side,
                wf[9 * p : 9 * p + 9].reshape(9 * CF, CF),
                preferred_element_type=F32,
            )
            pre = product if pre is None else pre + product
        sigma = 1.0 / (1.0 + jnp.exp(-pre))
        out_v[b] = (pre * sigma).astype(BF16)
        delta = cot_v[b].astype(F32) * (sigma * (1.0 + pre * (1.0 - sigma)))
        deltas[b // 2, :, b % 2] = delta.reshape(8, 64, CF)
        return carry

    for b in range(BLOCKS):
        fine_block(b, 0)
    write_out = pltpu.make_async_copy(out_v, out.at[0], out_sem)
    write_out.start()

    for half in range(BLOCKS // 2):
        turned = deltas[half].reshape(1024, CF).T.astype(BF16)
        for p in range(3):
            rows_p = slice(CF * p, CF * (p + 1))
            if p > 0:
                delta_t[half, rows_p, : CF * p] = jnp.zeros((CF, CF * p), BF16)
            delta_t[half, rows_p, CF * p : CF * p + 1024] = turned
            if p < 2:
                delta_t[half, rows_p, CF * p + 1024 :] = jnp.zeros((CF, CF * (2 - p)), BF16)

    def terms_of(first, count):
        terms = None
        for half in range(BLOCKS // 2):
            sides = jnp.concatenate(
                [cols[first + j, half].reshape(1280, CF) for j in range(count)], axis=1
            )
            product = jnp.dot(delta_t[half], sides, preferred_element_type=F32)
            terms = product if terms is None else terms + product
        return terms

    def pair_copy(k):
        return remote(
            pair_src.at[k],
            pair_dst.at[k],
            pair_send.at[k],
            pair_recv.at[k],
            scene=scene + 1 - 2 * core,
        )

    load_gorder.wait()

    def plane_copy(k, j):
        peer_x = lax.rem(my_x + far_x[j], n_x)
        source = plane_src.at[k, pl.ds(pl.multiple_of(CF * peer_x, CF), CF)]
        target = plane_dst.at[my_x * rows + row]
        if k == rows - 1 and j == n_x - 1:
            return pltpu.make_async_copy(source, target, plane_recv)
        return remote(
            source,
            target,
            plane_send.at[k * n_x + j],
            plane_recv,
            blk=peer_x * n_z + my_z,
            scene=2 * lax.rem(row + far_x[k], rows) + core,
        )

    def send_plane(k):
        pair_copy(k).wait_recv()
        total_k = (own[k] + pair_dst[k].astype(F32)).astype(BF16)
        filled = jnp.concatenate([total_k[3 * CF :], jnp.zeros((CF - REST, CF), BF16)], axis=0)
        parts = [total_k[CF * p : CF * (p + 1)] for p in range(3)] + [filled]
        ordered = lax.dot_general(
            order_gv[...],
            jnp.concatenate(parts, axis=1),
            (((1,), (1,)), ((), ())),
            preferred_element_type=F32,
        )
        plane_src[k] = ordered.astype(BF16)
        for j in range(n_x):
            plane_copy(k, j).start()

    rest[...] = terms_of(8, 1)
    for k in range(rows):
        target = lax.rem(row + far_x[k], rows)
        terms = terms_of(2 * target, 2)
        low, high = terms[:, :CF], terms[:, CF:]

        def rest_of(member):
            return rest[pl.ds(pl.multiple_of(REST * member, 16), REST), :]

        pair_src[k, : 3 * CF] = jnp.where(core == 0, high, low).astype(BF16)
        pair_src[k, 3 * CF :] = rest_of(2 * target + 1 - core).astype(BF16)
        pair_copy(k).start()
        own[k, : 3 * CF] = jnp.where(core == 0, low, high)
        own[k, 3 * CF :] = rest_of(2 * target + core)
        if k > 1:
            send_plane(k - 2)
    send_plane(rows - 2)
    send_plane(rows - 1)
    pltpu.make_async_copy(plane_dst, plane_dst, plane_recv).wait()
    plane_sum = jnp.sum(plane_dst[...].astype(F32), axis=0)
    shard_src[...] = plane_sum.astype(BF16).reshape(shard_src.shape)

    def shard_copy(k):
        peer = lax.rem(my_z + k, n_z)
        return remote(
            shard_src.at[peer],
            shards.at[my_z],
            shard_send.at[peer],
            shard_recv,
            blk=my_x * n_z + peer,
        )

    for k in far_z[:-1]:
        shard_copy(k).start()
    pltpu.make_async_copy(shard_src.at[my_z], shards.at[my_z], shard_recv).start()
    pltpu.make_async_copy(shards, shards, shard_recv).wait()
    done_src[...] = jnp.sum(shards[...].astype(F32), axis=0)

    def done_copy(k):
        peer = lax.rem(scene + k, n_scene)
        return remote(done_src, done.at[scene], done_send.at[peer], done_recv, scene=peer)

    pltpu.make_async_copy(done_src, done.at[scene], done_recv).start()

    def send_done(k, carry):
        done_copy(k).start()
        return carry

    for k in (4, 5, 3, 2, 6, 7, 1):
        send_done(k, 0)
    pltpu.make_async_copy(done, done, done_recv).wait()
    feat_right.wait_send()
    feat_left.wait_send()
    faces_right.wait_send()
    faces_left.wait_send()

    def sent_line(line, peer):
        @pl.when(peer != me)
        def _():
            meta_copy(line, peer).wait_send()
            line_copy(line, peer).wait_send()

    over_lines(sent_line)

    @pl.when(is_mid)
    def _():
        def step(k, carry):
            owner_copy(lax.rem(me + k, n_blk)).wait_send()
            return carry

        for k in range(1, n_blk):
            step(k, 0)

    for k in range(rows):
        pair_copy(k).wait_send()
    for k in range(rows):
        for j in range(n_x):
            if k < rows - 1 or j < n_x - 1:
                plane_copy(k, j).wait_send()
    for k in range(1, n_z):
        shard_copy(k).wait_send()

    def sent_done(k, carry):
        done_copy(k).wait_send()
        return carry

    lax.fori_loop(1, n_scene, sent_done, 0)
    write_out.wait()


def assemble(group, level_out, shares, out, grad, shares_v, out_v, grad_v, in_sem, out_sem, grad_sem):
    load = pltpu.make_async_copy(shares, shares_v, grad_sem.at[0])
    reads = [
        pltpu.make_async_copy(level_out.at[0, b], out_v.at[b], in_sem.at[b])
        for b in range(BLOCKS)
    ]
    writes = [
        pltpu.make_async_copy(out_v.at[b], out.at[0, b], out_sem.at[b]) for b in range(BLOCKS)
    ]
    load.start()
    for read in reads:
        read.start()
    load.wait()
    n_scene = shares_v.shape[0]
    for channel in range(grad_v.shape[1]):
        for p in range(3):
            for qr in range(n_scene):
                grad_v[9 * p + qr, channel, :] = shares_v[qr, channel * group + p, :]
        at = channel * group + 3
        last = jnp.concatenate(
            [shares_v[s, at : at + 1, :REST] for s in range(n_scene)], axis=1
        )
        for p in range(3):
            grad_v[9 * p + 8, channel : channel + 1, :] = last[:, CF * p : CF * (p + 1)]
    store = pltpu.make_async_copy(grad_v, grad, grad_sem.at[1])
    store.start()
    for read, write in zip(reads, writes):
        read.wait()
        write.start()
    store.wait()
    for write in writes:
        write.wait()


def body(n_blk, n_scene, feat, coarse_nbr, dest, fine_nbr, skip, cot, w_coarse, w_up, w_fine):
    group = 4
    shard = CF // n_blk
    rows = n_scene // 2
    n_x = n_blk // DEPTH
    any_spec = pl.BlockSpec(memory_space=pl.ANY)
    vmem = pltpu.VMEM
    dma = pltpu.SemaphoreType.DMA
    scratch = [
        pltpu.SMEM((1, BLOCKS, 4), jnp.int32),
        pltpu.SMEM((1, BLOCKS), jnp.int32),
        pltpu.SMEM((1, BLOCKS, 4), jnp.int32),
        vmem((3 * BLOCKS, 64, CC), BF16),
        vmem((TAPS, CC, CC), BF16),
        vmem((CC, CF), BF16),
        vmem((TAPS, CF, CF), BF16),
        vmem((BLOCKS, 512, CF), BF16),
        vmem((BLOCKS, 512, CF), BF16),
        vmem((864, 256), BF16),
        vmem((256, 256), BF16),
        vmem((96, 48), BF16),
        vmem((group * CF, group * CF), BF16),
        vmem((BLOCKS, 864, CC), BF16),
        vmem((16, CF), jnp.int32),
        vmem((n_blk, 16, CF), jnp.int32),
        vmem((LINES, 16, CF), BF16),
        vmem((n_blk, 16, CF), BF16),
        vmem((n_blk * 16, n_blk * 16), BF16),
        vmem((n_blk * 16 + 32, CF), BF16),
        vmem((LINES, 48, CF), BF16),
        vmem((LINES, 12, 8, CF), F32),
        vmem((3 * BLOCKS, 4, 64, CF), BF16),
        vmem((9, BLOCKS // 2, 10, 2, 64, CF), BF16),
        vmem((BLOCKS // 2, 8, 2, 64, CF), F32),
        vmem((BLOCKS // 2, 3 * CF, 1280), BF16),
        vmem((BLOCKS, 512, CF), BF16),
        vmem((3 * CF, CF), F32),
        vmem((rows, 3 * CF + REST, CF), F32),
        vmem((rows, 3 * CF + REST, CF), BF16),
        vmem((rows, 3 * CF + REST, CF), BF16),
        vmem((rows, group * CF, CF), BF16),
        vmem((rows * n_x, group * CF // n_x, CF), BF16),
        vmem((DEPTH, shard * group, CF), BF16),
        vmem((DEPTH, shard * group, CF), BF16),
        vmem((shard * group, CF), F32),
        dma((13,)),
        dma((4,)),
        dma((4,)),
        dma((LINES,)),
        dma,
        dma((LINES,)),
        dma,
        dma((n_blk,)),
        dma,
        dma((rows,)),
        dma((rows,)),
        dma((rows * n_x,)),
        dma,
        dma((DEPTH,)),
        dma,
        dma((n_scene,)),
        dma,
        dma,
        pltpu.SemaphoreType.REGULAR((3,)),
    ]
    level_out, shares = pl.pallas_call(
        functools.partial(kernel, n_blk, n_scene, group),
        out_shape=(
            jax.ShapeDtypeStruct((1, BLOCKS, 512, CF), BF16),
            jax.ShapeDtypeStruct((n_scene, shard * group, CF), F32),
        ),
        in_specs=[any_spec] * 13,
        out_specs=(any_spec, any_spec),
        scratch_shapes=scratch,
        compiler_params=pltpu.CompilerParams(
            collective_id=0, has_side_effects=True, vmem_limit_bytes=60 * 1024 * 1024
        ),
        name="decoder_level",
    )(
        feat,
        coarse_nbr,
        dest,
        fine_nbr,
        skip,
        cot,
        w_coarse,
        w_up,
        w_fine,
        jnp.asarray(coarse_selector(), BF16),
        jnp.asarray(line_order(), BF16),
        jnp.asarray(doubled_rows(), BF16),
        jnp.asarray(shard_order(group), BF16),
    )
    fine_out, gradient = pl.pallas_call(
        functools.partial(assemble, group),
        out_shape=(
            jax.ShapeDtypeStruct((1, BLOCKS, 512, CF), BF16),
            jax.ShapeDtypeStruct((TAPS, shard, CF), F32),
        ),
        in_specs=[any_spec, any_spec],
        out_specs=(any_spec, any_spec),
        scratch_shapes=[
            vmem((n_scene, shard * group, CF), F32),
            vmem((BLOCKS, 512, CF), BF16),
            vmem((TAPS, shard, CF), F32),
            dma((BLOCKS,)),
            dma((BLOCKS,)),
            dma((2,)),
        ],
        name="assemble",
    )(level_out, shares)
    return fine_out, jnp.transpose(gradient, (1, 0, 2))


def solution(mesh):
    in_specs = (
        P("scene", "blk", None, None),
        P("scene", "blk", None),
        P("scene", "blk"),
        P("scene", "blk", None),
        P("scene", "blk", None, None),
        P("scene", "blk", None, None),
        P(),
        P(),
        P(),
    )
    out_specs = (P("scene", "blk", None, None), P("blk", None, None))
    return jax.shard_map(
        functools.partial(body, mesh.shape["blk"], mesh.shape["scene"]),
        mesh=mesh,
        in_specs=in_specs,
        out_specs=out_specs,
        check_vma=False,
    )
```
